512 devices in a mesh: seq: 64 (over z, x_hi, core), head: 8 (over x_lo, y).
Axes of the slice: x: 4 (x_hi: 2, x_lo: 2; x = x_hi * 2 + x_lo), y: 4, z: 16, core: 2. Of those that a mesh axis runs over, the one named last changes fastest.
Arguments:
- events: bfloat16 [16384, 1024], P('seq'), may hold values from -60 to 60
- out_grad: bfloat16 [16384, 1024], P('seq', 'head'), may hold values from -16 to 16
- saved_attn: bfloat16 [16384, 1024], P('seq', 'head'), may hold values from -0.119628906 to 0.119628906
- in_weight: bfloat16 [1024, 4096], P(None, 'head'), may hold values from -0.1875 to 0.1875
- out_weight: bfloat16 [1024, 1024], P(None, 'head'), may hold values from -0.1875 to 0.1875
- lengths: int32 [16], replicated, may hold values from 1 to 4096, 16384 in all
Outputs:
- grad_in: bfloat16 [16384, 1024], P('seq', 'head')
- grad_w1: float32 [1024, 4096], P('seq', 'head')
- grad_w2: float32 [1024, 1024], P('seq', 'head')
The draws below stay inside these ranges and needn't reach their ends.
Inputs may be any that keep to these rules, and one draw needn't show every extreme that they name: The 16 lengths sum to 16384 and the longest is exactly 4096.
All inputs are finite; a program needn't handle non-finite values.
Results may differ from the reference program's by a relative error of at most 0.0077.
Values may be sent and summed in bfloat16 or wider, within the bound.
A program may use at most 64 MiB of HBM per device.

```python
import math
import jax
import jax.numpy as jnp
import numpy as np
from jax import lax

D = 1024
H = 8
HEAD_DIM = 128
TOK_DEV = 256
NSEQ = 16
TOKENS = 16384
MOST = 4096
SPAN = 16


def draw_events(key, part):
    key = jax.random.fold_in(key, 11)
    first = jax.random.fold_in(key, 0)
    columns = 1.0 + 2.0 * jnp.arange(D, dtype=jnp.float32) / D
    base = jax.random.normal(first, (TOKENS, D), jnp.float32)
    base = jnp.clip(base, -6.0, 6.0)
    return (base * columns[None, :]).astype(jnp.bfloat16)


def spiked(array, key, source, target, shards_of, factor):
    def block_of(dim):
        return (jnp.arange(array.shape[dim]) // (array.shape[dim] // shards_of)).reshape((-1,) + (1,) * (array.ndim - 1 - dim))

    first = jax.random.permutation(key, shards_of)[block_of(target)]
    other_side = (block_of(target) + shards_of // 2) % shards_of
    return jnp.where((block_of(source) == first) | (block_of(source) == other_side), factor * array, array)


def block_scale(rng, shape, pieces, smallest, largest):
    gain, own = 1.0, jax.random.fold_in(rng, 6)
    for dim, shards_of in pieces:
        draws = jnp.exp(jax.random.uniform(jax.random.fold_in(own, dim), (shards_of,), jnp.float32, smallest / len(pieces), largest / len(pieces)))
        gain = gain * jnp.repeat(draws, shape[dim] // shards_of).reshape([-1 if axis == dim else 1 for axis in range(len(shape))])
    return gain


def profile(number_of, total, limit, slope):
    loads = [(1 << 20) // math.isqrt(standing ** slope) + 1 for standing in range(2, number_of + 1)]
    rest, given = total - limit - (number_of - 1), [1] * (number_of - 1)
    while rest > 0:
        candidates = [i for i in range(number_of - 1) if given[i] < limit]
        mass, remaining = sum([loads[i] for i in candidates]), rest
        for i in candidates:
            more = min(limit - given[i], max(1, remaining * loads[i] // mass), rest)
            given[i] = given[i] + more
            rest = rest - more
    return np.array([limit] + given)


def uneven_parts(rng, number_of, total, bound, lean):
    if number_of == 2:
        one = jax.random.randint(rng, (), max(1, total - bound), min(bound, total - 1) + 1)
        return jnp.stack([one, total - one])
    sizes = jnp.asarray(profile(number_of, total, bound, lean), jnp.int32)
    pairs = (number_of - 1) // 2
    donor, receiver = sizes[1:1 + 2 * pairs:2], sizes[2:2 + 2 * pairs:2]
    slack = jnp.minimum(donor - 1, bound - receiver)
    moved = jax.random.randint(jax.random.fold_in(rng, 1), (pairs,), 0, 1 << 20) % (slack + 1)
    sizes = sizes.at[1:1 + 2 * pairs:2].set(donor - moved).at[2:2 + 2 * pairs:2].set(receiver + moved)
    return sizes[jax.random.permutation(jax.random.fold_in(rng, 2), number_of)]


def scatter_about(rng, shape, width, bound, pieces=(), held_as=jnp.bfloat16):
    loudness = block_scale(rng, shape, pieces, -0.22, 0.18) if pieces else 1.0
    entries = jax.random.normal(rng, shape, jnp.float32) * width * loudness
    return jnp.minimum(jnp.maximum(entries, -bound), bound).astype(held_as)


def bell_draw_with(own_key, dims, scale, reach, pieces, heavy, kind=jnp.bfloat16):
    values = scale * jax.random.normal(own_key, dims, jnp.float32)
    if pieces:
        values = values * block_scale(own_key, dims, pieces, -0.22, 0.18)
    return jnp.clip(spiked(values, jax.random.fold_in(own_key, 3), *heavy), -reach, reach).astype(kind)


def setup_inputs(seed: int = 0) -> dict:
    streams_of = jax.random.split(jax.random.key(seed), 7)
    events = draw_events(jax.random.fold_in(streams_of[6], 71), 0)
    out_grad = bell_draw_with(streams_of[1], (TOKENS, D), 1.0, 16.0, ((0, 64), (1, 8)), (0, 1, 64, 4.0))
    saved_attn = scatter_about(streams_of[2], (TOKENS, H * HEAD_DIM), 0.02, 0.119628906, ((0, 64), (1, 8)))
    in_weight = scatter_about(streams_of[3], (D, 4 * H * HEAD_DIM), D ** -0.5, 0.1875, ((1, 8),))
    out_weight = scatter_about(streams_of[4], (D, H * HEAD_DIM), (H * HEAD_DIM) ** -0.5, 0.1875, ((1, 8),))
    lengths = uneven_parts(streams_of[5], NSEQ, TOKENS, MOST, 2).astype(jnp.int32)
    return {"events": events, "out_grad": out_grad, "saved_attn": saved_attn, "in_weight": in_weight, "out_weight": out_weight, "lengths": lengths}


EPS = 1e-05

def silu_slope(value):
    sig = jax.nn.sigmoid(value)
    return sig * (1.0 + value * (1.0 - sig))

def segment_of(position, lengths):
    ends = jnp.cumsum(lengths)
    return lax.optimization_barrier(jnp.sum((position[:, None] >= ends[None, :]).astype(jnp.int32), axis=1))

def reference(events, out_grad, saved_attn, in_weight, out_weight, lengths):
    f32 = jnp.float32
    bf = jnp.bfloat16
    halfway = TOKENS // 2
    events = jnp.roll(events, halfway, axis=0)
    out_grad = jnp.roll(out_grad, halfway, axis=0)
    saved_attn = jnp.roll(saved_attn, halfway, axis=0)
    rows = events.astype(f32)
    cent = rows - lax.optimization_barrier(jnp.mean(rows, axis=1, keepdims=True))
    rstd = lax.rsqrt(lax.optimization_barrier(jnp.mean(cent * cent, axis=1, keepdims=True)) + EPS)
    normed = cent * rstd
    normed_b = normed.astype(bf)
    proj = jnp.dot(normed_b, in_weight, preferred_element_type=f32)
    act = jax.nn.silu(proj).astype(bf).reshape(TOKENS, H, 4, HEAD_DIM)
    upart = act[:, :, 0]
    values = act[:, :, 1]
    queries = act[:, :, 2]
    keys = act[:, :, 3]
    dout = jnp.dot(out_grad, out_weight, preferred_element_type=f32).reshape(TOKENS, H, HEAD_DIM)
    attn = saved_attn.astype(f32).reshape(TOKENS, H, HEAD_DIM)
    acent = attn - lax.optimization_barrier(jnp.mean(attn, axis=2, keepdims=True))
    arstd = lax.rsqrt(lax.optimization_barrier(jnp.mean(acent * acent, axis=2, keepdims=True)) + EPS)
    ahat = acent * arstd
    upf = upart.astype(f32)
    gated = (ahat * upf).astype(bf).reshape(TOKENS, H * HEAD_DIM)
    grad_scale = 1.0 / math.sqrt(TOKENS)
    grad_w2 = jnp.dot(out_grad.T, gated, preferred_element_type=f32) * grad_scale
    grad_u = dout * ahat
    dnorm = dout * upf
    grad_attn = ((dnorm - lax.optimization_barrier(jnp.mean(dnorm, axis=2, keepdims=True)) - ahat * lax.optimization_barrier(jnp.mean(dnorm * ahat, axis=2, keepdims=True))) * arstd).astype(bf)
    positions = jnp.arange(TOKENS, dtype=jnp.int32)
    segs = segment_of(positions, lengths)
    pad = SPAN * TOK_DEV
    window = pad + TOK_DEV
    keys_p = jnp.concatenate([jnp.zeros((pad, H, HEAD_DIM), bf), keys], axis=0)
    values_p = jnp.concatenate([jnp.zeros((pad, H, HEAD_DIM), bf), values], axis=0)
    pos_p = jnp.concatenate([-jnp.ones((pad,), jnp.int32), positions], axis=0)
    seg_p = jnp.concatenate([-jnp.ones((pad,), jnp.int32), segs.astype(jnp.int32)], axis=0)
    scale = 1.0 / math.sqrt(HEAD_DIM)
    norm = float(MOST)

    def block(carry, index):
        grad_k_all, grad_v_all = carry
        start = (index * TOK_DEV).astype(jnp.int32)
        qblk = lax.dynamic_slice_in_dim(queries, start, TOK_DEV, 0).astype(f32)
        zblk = lax.dynamic_slice_in_dim(grad_attn, start, TOK_DEV, 0).astype(f32)
        qpos = lax.dynamic_slice_in_dim(positions, start, TOK_DEV, 0)
        qseg = lax.dynamic_slice_in_dim(segs, start, TOK_DEV, 0)
        kblk = lax.dynamic_slice_in_dim(keys_p, start, window, 0).astype(f32)
        vblk = lax.dynamic_slice_in_dim(values_p, start, window, 0).astype(f32)
        kpos = lax.dynamic_slice_in_dim(pos_p, start, window, 0)
        kseg = lax.dynamic_slice_in_dim(seg_p, start, window, 0)
        mask = (qseg[:, None] == kseg[None, :]) & (kpos[None, :] <= qpos[:, None])
        scores = jnp.einsum('qhd,khd->hqk', qblk, kblk) * scale
        sig = jax.nn.sigmoid(scores)
        weights = jnp.where(mask[None], scores * sig / norm, 0.0).astype(bf).astype(f32)
        dprob = jnp.einsum('qhd,khd->hqk', zblk, vblk)
        dscore = jnp.where(mask[None], dprob * sig * (1.0 + scores * (1.0 - sig)) / norm, 0.0).astype(bf).astype(f32)
        grad_q = jnp.einsum('hqk,khd->qhd', dscore, kblk) * scale
        grad_k = jnp.einsum('hqk,qhd->khd', dscore, qblk) * scale
        grad_v = jnp.einsum('hqk,qhd->khd', weights, zblk)
        old_k = lax.dynamic_slice_in_dim(grad_k_all, start, window, 0)
        old_v = lax.dynamic_slice_in_dim(grad_v_all, start, window, 0)
        grad_k_all = lax.dynamic_update_slice_in_dim(grad_k_all, old_k + grad_k, start, 0)
        grad_v_all = lax.dynamic_update_slice_in_dim(grad_v_all, old_v + grad_v, start, 0)
        return ((grad_k_all, grad_v_all), grad_q)
    start_k = jnp.zeros((pad + TOKENS, H, HEAD_DIM), f32)
    (grad_k_all, grad_v_all), grad_q_blocks = lax.scan(block, (start_k, start_k), jnp.arange(TOKENS // TOK_DEV, dtype=jnp.int32))
    grad_q = grad_q_blocks.reshape(TOKENS, H, HEAD_DIM)
    grad_k = grad_k_all[pad:]
    grad_v = grad_v_all[pad:]
    stacked = jnp.stack((grad_u, grad_v, grad_q, grad_k), axis=2)
    dproj = (stacked * silu_slope(proj.reshape(TOKENS, H, 4, HEAD_DIM))).astype(bf).reshape(TOKENS, 4 * H * HEAD_DIM)
    grad_w1 = jnp.dot(normed_b.T, dproj, preferred_element_type=f32) * grad_scale
    dnormed = jnp.dot(dproj, in_weight.T, preferred_element_type=f32)
    back = (dnormed - lax.optimization_barrier(jnp.mean(dnormed, axis=1, keepdims=True)) - normed * lax.optimization_barrier(jnp.mean(dnormed * normed, axis=1, keepdims=True))) * rstd
    grad_in = (out_grad.astype(f32) + back).astype(bf)
    grad_in = jnp.roll(grad_in, -halfway, axis=0)
    return (grad_in, grad_w1, grad_w2)
```

```python
import math

import jax
import jax.numpy as jnp
from jax import lax
from jax.experimental import pallas as pl
from jax.experimental.pallas import tpu as pltpu
from jax.sharding import PartitionSpec as P

HEADS = 8
HD = 128
TOK = 256
WIDTH = 1024
PLANES = 16
NSEQ = 16
REACH = 4
MOST = 4096.0
EPS = 1e-05
SCALE = 1.0 / math.sqrt(HD)
GRAD_SCALE = 1.0 / 128.0
MESH = pl.DeviceIdType.MESH
F32 = jnp.float32
BF16 = jnp.bfloat16
NEAR_LAST = (8, 7, 9, 6, 10, 5, 11, 4, 12, 3, 13, 2, 14, 1, 15)


def nn(a, b):
    return jnp.dot(a, b, preferred_element_type=F32)


def nt(a, b):
    return lax.dot_general(a, b, (((1,), (1,)), ((), ())), preferred_element_type=F32)


def tn(a, b):
    return lax.dot_general(a, b, (((0,), (0,)), ((), ())), preferred_element_type=F32)


def push(src, dst, sent, came, device):
    return pltpu.make_async_remote_copy(
        src_ref=src,
        dst_ref=dst,
        send_sem=sent,
        recv_sem=came,
        device_id=device,
        device_id_type=MESH,
    )


def kernel(
    ev, og, sa, wi, wo, lens, gi, g1, g2,
    n8, nb, ntr, rsd, slope, upart, ahat_s, arstd_s, dproj,
    fg, qa, doa, kva, kvg, dqs, dqr,
    kvs1, kvr1, kvs2, kvr2,
    ge, ge1, ga1, ge2, ga2, ge3,
    gl, gl1, gb1, gl2, gb2, gl3,
    ps, pr, own, st, sr,
    fg_s, fg_r, q_s, q_r, do_s, do_r, kv_s, kv_r, dq_s, dq_r, kx_s, kx_r,
    e12_s, e12_r, e3_s, e3_r, l12_s, l12_r, l3_s, l3_r, p_s, p_r, t_s, t_r,
):
    s = lax.axis_index("seq")
    h = lax.axis_index("head")
    z = s // 4
    xh = (s // 2) % 2
    c = s % 2

    def at_z(i):
        return (((z + i) % PLANES) * 4 + xh * 2 + c, h)

    def in_plane(i):
        return (z * 4 + ((xh + i // 2) % 2) * 2 + (c + i % 2) % 2, h)

    def at_head(i):
        return (s, (h + i) % HEADS)

    barrier = pltpu.get_barrier_semaphore()
    for i in range(1, HEADS):
        pl.semaphore_signal(barrier, inc=1, device_id=at_head(i), device_id_type=MESH)
    for i in range(1, 4):
        pl.semaphore_signal(barrier, inc=1, device_id=in_plane(i), device_id_type=MESH)
    for i in range(1, PLANES):
        pl.semaphore_signal(barrier, inc=1, device_id=at_z(i), device_id_type=MESH)

    def norm_rows(i, carry):
        r = pl.multiple_of(i * 32, 32)
        x = ev[pl.ds(r, 32), :].astype(F32)
        cent = x - jnp.mean(x, axis=1, keepdims=True)
        rstd = lax.rsqrt(jnp.mean(cent * cent, axis=1, keepdims=True) + EPS)
        normed = cent * rstd
        nb[pl.ds(r, 32), :] = normed.astype(BF16)
        for j in range(HEADS):
            n8[j, pl.ds(r, 32), :] = normed[:, j * HD : (j + 1) * HD]
        rsd[pl.ds(r, 32), :] = jnp.broadcast_to(rstd, (32, HD))
        return carry

    lax.fori_loop(0, TOK // 32, norm_rows, 0)

    pl.semaphore_wait(barrier, HEADS - 1 + 3 + PLANES - 1)
    fg_copies = [
        push(og, fg.at[i], fg_s.at[i], fg_r.at[i], at_head(i)) for i in range(1, HEADS)
    ]
    for copy in fg_copies:
        copy.start()

    for part in (2, 3, 1, 0):
        proj = nn(nb[...], wi[:, part * HD : (part + 1) * HD])
        sig = 0.5 * jnp.tanh(0.5 * proj) + 0.5
        act = (proj * sig).astype(BF16)
        slope[part] = sig * (1.0 + proj * (1.0 - sig))
        if part == 0:
            upart[...] = act.astype(F32)
        elif part == 1:
            kva[0, 1] = act
        elif part == 2:
            qa[0] = act
        else:
            kva[0, 0] = act

    q_copies = [
        push(qa.at[0], qa.at[d], q_s.at[d], q_r.at[d], at_z(PLANES - d))
        for d in range(REACH, 0, -1)
    ]
    kv_copies = [
        push(kva.at[0], kva.at[i], kv_s.at[i], kv_r.at[i], in_plane(i)) for i in (3, 2, 1)
    ]
    for copy in kv_copies + q_copies:
        copy.start()

    attn = sa[...].astype(F32)
    cent = attn - jnp.mean(attn, axis=1, keepdims=True)
    arstd = lax.rsqrt(jnp.mean(cent * cent, axis=1, keepdims=True) + EPS)
    ahat_s[...] = cent * arstd
    arstd_s[...] = jnp.broadcast_to(arstd, (TOK, HD))
    kvg[...] = jnp.zeros_like(kvg)

    def turn_columns(j, carry):
        ntr[pl.ds(pl.multiple_of(j * HD, HD), HD), :] = n8[j].T.astype(BF16)
        return carry

    lax.fori_loop(0, HEADS, turn_columns, 0)

    dout = nn(og[...], wo[pl.ds(pl.multiple_of(h * HD, HD), HD), :])
    for i in range(1, HEADS):
        fg_copies[i - 1].wait_recv()
        row = pl.multiple_of(((h + HEADS - i) % HEADS) * HD, HD)
        dout += nn(fg[i], wo[pl.ds(row, HD), :])
    ahat = ahat_s[...]
    dnorm = dout * upart[...]
    doa[0] = (
        (
            dnorm
            - jnp.mean(dnorm, axis=1, keepdims=True)
            - ahat * jnp.mean(dnorm * ahat, axis=1, keepdims=True)
        )
        * arstd_s[...]
    ).astype(BF16)
    do_copies = [
        push(doa.at[0], doa.at[d], do_s.at[d], do_r.at[d], at_z(PLANES - d))
        for d in range(REACH, 0, -1)
    ]
    for copy in do_copies:
        copy.start()

    dproj[:, 0:HD] = (dout * ahat * slope[0]).astype(BF16)
    gated = (ahat * upart[...]).astype(BF16)
    ge[:, :, :, 0:HD] = (nn(ntr[...], dproj[:, 0:HD])).astype(BF16).reshape(32, 2, 16, HD)
    for i in range(HEADS):
        block = pl.ds(((h + HEADS - i) % HEADS) * 4, 4)
        rows = og[...] if i == 0 else fg[i]
        ge[block, :, :, HD : 2 * HD] = tn(rows, gated).astype(BF16).reshape(4, 2, 16, HD)

    def sum_parts(whole, into, over):
        one = push(whole.at[:, 1 - c], into, over[0].at[0], over[1].at[0], in_plane(1))
        return one

    def add_first(whole, came, kept):
        def step(i, carry):
            kept[i] = (
                whole[pl.ds(2 * i, 2), c].astype(F32) + came[pl.ds(2 * i, 2)].astype(F32)
            ).astype(BF16)
            return carry

        lax.fori_loop(0, PLANES, step, 0)

    def sum_across(kept, into, over):
        return push(kept.at[:, 1 - xh], into, over[0].at[1], over[1].at[1], in_plane(2))

    def add_second(kept, came, final):
        def step(i, carry):
            final[i] = (kept[i, xh].astype(F32) + came[i].astype(F32)).astype(BF16)
            return carry

        lax.fori_loop(0, PLANES, step, 0)

    def sum_planes(final, into, over):
        return [
            push(final.at[(z + i) % PLANES], into.at[i], over[0].at[i], over[1].at[i], at_z(i))
            for i in NEAR_LAST
        ]

    def add_third(final, came):
        total = final[z].astype(F32)
        for i in range(1, PLANES):
            total += came[i].astype(F32)
        return total * GRAD_SCALE

    e_first = sum_parts(ge, ge1, (e12_s, e12_r))
    e_first.start()

    ends = []
    run = 0
    for i in range(NSEQ):
        run = run + lens[i]
        ends.append(run)
    own_plane = (z + PLANES // 2) % PLANES

    for copy in kv_copies:
        copy.wait_recv()

    def attend(turn, carry):
        d = jnp.where(turn == 0, 0, REACH + 1 - turn)

        @pl.when(turn > 0)
        def _():
            push(qa.at[0], qa.at[d], q_s.at[d], q_r.at[d], at_z(d)).wait_recv()
            push(doa.at[0], doa.at[d], do_s.at[d], do_r.at[d], at_z(d)).wait_recv()

        queries = qa[d]
        upstream = doa[d]
        lane = lax.broadcasted_iota(jnp.int32, (1, TOK), 1)
        qpos = ((own_plane + d) % PLANES) * 1024 + xh * 512 + c * 256 + lane
        first = jnp.zeros((1, TOK), jnp.int32)
        for end in ends:
            first = jnp.maximum(first, jnp.where(qpos >= end, end, 0))

        def block(i, grad_q):
            keys = kva[i, 0]
            values = kva[i, 1]
            kpos = (
                own_plane * 1024
                + ((xh + i // 2) % 2) * 512
                + ((c + i) % 2) * 256
                + lax.broadcasted_iota(jnp.int32, (TOK, TOK), 0)
            )
            mask = (kpos <= qpos) & (kpos >= first)
            scores = nt(keys, queries) * SCALE
            sig = 0.5 * jnp.tanh(0.5 * scores) + 0.5
            weight = scores * sig
            dprob = nt(values, upstream)
            dscore = jnp.where(mask, dprob * (sig + weight * (1.0 - sig)), 0.0).astype(BF16)
            weight = jnp.where(mask, weight, 0.0).astype(BF16)
            kvg[i, 0] += nn(dscore, queries)
            kvg[i, 1] += nn(weight, upstream)
            return grad_q + tn(dscore, keys)

        grad_q = lax.fori_loop(0, 4, block, jnp.zeros((TOK, HD), F32))
        dqs[d] = grad_q.astype(BF16)

        @pl.when(turn > 0)
        def _():
            push(dqs.at[d], dqr.at[d], dq_s.at[d], dq_r.at[d], at_z(d)).start()

        return carry

    lax.fori_loop(0, REACH + 1, attend, 0)

    for j in range(2):
        other = 2 * j + 1
        kvs1[j] = kvg[other].astype(BF16)
    k_first = push(kvs1, kvr1, kx_s.at[0], kx_r.at[0], in_plane(1))
    k_first.start()

    e_first.wait_recv()
    add_first(ge, ge1, ga1)
    e_second = sum_across(ga1, ge2, (e12_s, e12_r))
    e_second.start()

    k_first.wait_recv()
    kvs2[...] = (kvg[2] + kvr1[1].astype(F32)).astype(BF16)
    k_second = push(kvs2, kvr2, kx_s.at[1], kx_r.at[1], in_plane(2))
    k_second.start()

    dq_copies = [
        push(dqs.at[d], dqr.at[d], dq_s.at[d], dq_r.at[d], at_z(d)) for d in range(1, REACH + 1)
    ]
    grad_q = dqs[0].astype(F32)
    for d in range(REACH, 0, -1):
        dq_copies[d - 1].wait_recv()
        grad_q += dqr[d].astype(F32)
    dproj[:, 2 * HD : 3 * HD] = (grad_q * (SCALE / MOST) * slope[2]).astype(BF16)
    gl[:, :, :, HD : 2 * HD] = (
        nn(ntr[...], dproj[:, 2 * HD : 3 * HD]).astype(BF16).reshape(32, 2, 16, HD)
    )

    e_second.wait_recv()
    add_second(ga1, ge2, ga2)
    e_third = sum_planes(ga2, ge3, (e3_s, e3_r))
    for copy in e_third:
        copy.start()

    k_second.wait_recv()
    grad_k = kvg[0, 0] + kvr1[0, 0].astype(F32) + kvr2[0].astype(F32)
    grad_v = kvg[0, 1] + kvr1[0, 1].astype(F32) + kvr2[1].astype(F32)
    dproj[:, 3 * HD :] = (grad_k * (SCALE / MOST) * slope[3]).astype(BF16)
    dproj[:, HD : 2 * HD] = (grad_v * (1.0 / MOST) * slope[1]).astype(BF16)
    gl[:, :, :, 2 * HD :] = nn(ntr[...], dproj[:, 3 * HD :]).astype(BF16).reshape(32, 2, 16, HD)
    gl[:, :, :, 0:HD] = nn(ntr[...], dproj[:, HD : 2 * HD]).astype(BF16).reshape(32, 2, 16, HD)
    l_first = sum_parts(gl, gl1, (l12_s, l12_r))
    l_first.start()

    total = jnp.zeros((TOK, HD), F32)
    along = jnp.zeros((TOK, HD), F32)
    p_copies = []
    for i in (6, 2, 7, 5, 3, 1, 4, 0):
        hh = (h + i) % HEADS
        part = nt(dproj[...], wi[pl.ds(pl.multiple_of(hh * HD, HD), HD), :])
        total += part
        along += part * n8[hh]
        if i:
            ps[i] = part.astype(BF16)
            copy = push(ps.at[i], pr.at[i], p_s.at[i], p_r.at[i], at_head(i))
            copy.start()
            p_copies.append((i, copy))
        else:
            own[...] = part
    lane = lax.broadcasted_iota(jnp.int32, (TOK, HD), 1)
    both = jnp.where(
        lane == 0,
        jnp.sum(total, axis=1, keepdims=True),
        jnp.where(lane == 1, jnp.sum(along, axis=1, keepdims=True), 0.0),
    )
    st[...] = both.T[0:8, :]
    t_copies = [
        push(st, sr.at[i], t_s.at[i], t_r.at[i], at_head(i)) for i in range(1, HEADS)
    ]
    for copy in t_copies:
        copy.start()

    l_first.wait_recv()
    add_first(gl, gl1, gb1)
    l_second = sum_across(gb1, gl2, (l12_s, l12_r))
    l_second.start()

    for copy in e_third:
        copy.wait_recv()
    early = add_third(ga2, ge3)
    g1[:, 0:HD] = early[:, 0:HD]
    g2[...] = early[:, HD:]

    l_second.wait_recv()
    add_second(gb1, gl2, gb2)
    l_third = sum_planes(gb2, gl3, (l3_s, l3_r))
    for copy in l_third:
        copy.start()

    summed = own[...]
    for i, copy in p_copies:
        copy.wait_recv()
        summed += pr[i].astype(F32)
    stats = st[...]
    for i in range(1, HEADS):
        t_copies[i - 1].wait_recv()
        stats += sr[i]
    wide = jnp.concatenate([stats, jnp.zeros((HD - 8, TOK), F32)], axis=0).T * (1.0 / WIDTH)
    back = (summed - wide[:, 0:1] - n8[h] * wide[:, 1:2]) * rsd[...]
    gi[...] = (og[...].astype(F32) + back).astype(BF16)

    for copy in l_third:
        copy.wait_recv()
    late = add_third(gb2, gl3)
    g1[:, HD:] = late

    for copy in (
        fg_copies + q_copies + kv_copies + do_copies + dq_copies + e_third + l_third + t_copies
    ):
        copy.wait_send()
    for i, copy in p_copies:
        copy.wait_send()
    for copy in (e_first, e_second, k_first, k_second, l_first, l_second):
        copy.wait_send()


def rows_of(columns):
    return [
        pltpu.VMEM((32, 2, 16, columns), BF16),
        pltpu.VMEM((32, 16, columns), BF16),
        pltpu.VMEM((16, 2, 16, columns), BF16),
        pltpu.VMEM((16, 16, columns), BF16),
        pltpu.VMEM((16, 16, columns), BF16),
        pltpu.VMEM((16, 16, columns), BF16),
    ]


def per_device(events, out_grad, saved_attn, in_weight, out_weight, lengths):
    tile = (TOK, HD)
    vmem = pl.BlockSpec(memory_space=pltpu.VMEM)
    dma = pltpu.SemaphoreType.DMA
    scratch = [
        pltpu.VMEM((HEADS,) + tile, F32),
        pltpu.VMEM((TOK, WIDTH), BF16),
        pltpu.VMEM((WIDTH, TOK), BF16),
        pltpu.VMEM(tile, F32),
        pltpu.VMEM((4,) + tile, F32),
        pltpu.VMEM(tile, F32),
        pltpu.VMEM(tile, F32),
        pltpu.VMEM(tile, F32),
        pltpu.VMEM((TOK, 4 * HD), BF16),
        pltpu.VMEM((HEADS,) + tile, BF16),
        pltpu.VMEM((REACH + 1,) + tile, BF16),
        pltpu.VMEM((REACH + 1,) + tile, BF16),
        pltpu.VMEM((4, 2) + tile, BF16),
        pltpu.VMEM((4, 2) + tile, F32),
        pltpu.VMEM((REACH + 1,) + tile, BF16),
        pltpu.VMEM((REACH + 1,) + tile, BF16),
        pltpu.VMEM((2, 2) + tile, BF16),
        pltpu.VMEM((2, 2) + tile, BF16),
        pltpu.VMEM((2,) + tile, BF16),
        pltpu.VMEM((2,) + tile, BF16),
        *rows_of(2 * HD),
        *rows_of(3 * HD),
        pltpu.VMEM((HEADS,) + tile, BF16),
        pltpu.VMEM((HEADS,) + tile, BF16),
        pltpu.VMEM(tile, F32),
        pltpu.VMEM((8, TOK), F32),
        pltpu.VMEM((HEADS, 8, TOK), F32),
    ]
    counts = (8, 8, 5, 5, 5, 5, 4, 4, 5, 5, 2, 2, 2, 2, 16, 16, 2, 2, 16, 16, 8, 8, 8, 8)
    scratch += [dma((n,)) for n in counts]
    return pl.pallas_call(
        kernel,
        out_shape=(
            jax.ShapeDtypeStruct(tile, BF16),
            jax.ShapeDtypeStruct((16, 4 * HD), F32),
            jax.ShapeDtypeStruct((16, HD), F32),
        ),
        in_specs=[vmem] * 5 + [pl.BlockSpec(memory_space=pltpu.SMEM)],
        out_specs=(vmem,) * 3,
        scratch_shapes=scratch,
        compiler_params=pltpu.CompilerParams(
            collective_id=0, has_side_effects=True, vmem_limit_bytes=48 * 2**20
        ),
        name="layer_backward",
    )(events, out_grad, saved_attn, in_weight, out_weight, lengths)


def solution(mesh):
    return jax.shard_map(
        per_device,
        mesh=mesh,
        in_specs=(
            P("seq", None),
            P("seq", "head"),
            P("seq", "head"),
            P(None, "head"),
            P(None, "head"),
            P(),
        ),
        out_specs=(P("seq", "head"), P("seq", "head"), P("seq", "head")),
        check_vma=False,
    )
```

```python
import math

import jax
import jax.numpy as jnp
from jax import lax
from jax.experimental import pallas as pl
from jax.experimental.pallas import tpu as pltpu
from jax.sharding import PartitionSpec as P

HEADS = 8
HD = 128
TOK = 256
WIDTH = 1024
PLANES = 16
NSEQ = 16
REACH = 4
MOST = 4096.0
EPS = 1e-05
SCALE = 1.0 / math.sqrt(HD)
GRAD_SCALE = 1.0 / 128.0
MESH = pl.DeviceIdType.MESH
F32 = jnp.float32
BF16 = jnp.bfloat16
NEAR_LAST = (8, 7, 9, 6, 10, 5, 11, 4, 12, 3, 13, 2, 14, 1, 15)


def nn(a, b):
    return jnp.dot(a, b, preferred_element_type=F32)


def nt(a, b):
    return lax.dot_general(a, b, (((1,), (1,)), ((), ())), preferred_element_type=F32)


def tn(a, b):
    return lax.dot_general(a, b, (((0,), (0,)), ((), ())), preferred_element_type=F32)


def push(src, dst, sent, came, device):
    return pltpu.make_async_remote_copy(
        src_ref=src,
        dst_ref=dst,
        send_sem=sent,
        recv_sem=came,
        device_id=device,
        device_id_type=MESH,
    )


def kernel(
    ev_h, og_h, sa_h, wi_h, wo_h, lens_h, gi, g1, g2,
    ev, sa, wi, wo, lens,
    n8, nb, ntr, rsd, slope, upart, ahat_s, arstd_s, dproj,
    fg, qa, doa, kva, ktr, wts, slp, kvg, dqs, dqr,
    kvs1, kvr1, kvs2, kvr2,
    ge, ge1, ga1, ge2, ga2, ge3,
    gl, gl1, gb1, gl2, gb2, gl3,
    ps, pr, own, st, sr,
    in_s, near,
    fg_s, fg_r, q_s, q_r, do_s, do_r, kv_s, kv_r, dq_s, dq_r, kx_s, kx_r,
    e12_s, e12_r, e3_s, e3_r, l12_s, l12_r, l3_s, l3_r, p_s, p_r, t_s, t_r,
):
    s = lax.axis_index("seq")
    h = lax.axis_index("head")
    z = s // 4
    xh = (s // 2) % 2
    c = s % 2

    def at_z(i):
        return (((z + i) % PLANES) * 4 + xh * 2 + c, h)

    def in_plane(i):
        return (z * 4 + ((xh + i // 2) % 2) * 2 + (c + i % 2) % 2, h)

    def at_head(i):
        return (s, (h + i) % HEADS)

    barrier = pltpu.get_barrier_semaphore()
    for i in range(1, HEADS):
        pl.semaphore_signal(barrier, inc=1, device_id=at_head(i), device_id_type=MESH)
    for i in range(1, 4):
        pl.semaphore_signal(barrier, inc=1, device_id=in_plane(i), device_id_type=MESH)
    for i in (1, PLANES - 1):
        pl.semaphore_signal(barrier, inc=1, device_id=at_z(i), device_id_type=MESH)

    def greet(level, distance):
        for i in (distance, PLANES - distance):
            pl.semaphore_signal(
                near.at[level], inc=1, device_id=at_z(i), device_id_type=MESH
            )

    loads = [
        pltpu.make_async_copy(src, dst, in_s.at[i])
        for i, (src, dst) in enumerate(
            ((og_h, fg.at[0]), (ev_h, ev), (wi_h, wi), (wo_h, wo), (sa_h, sa), (lens_h, lens))
        )
    ]
    for copy in loads:
        copy.start()

    def norm_rows(i, carry):
        r = pl.multiple_of(i * 64, 64)
        x = ev[pl.ds(r, 64), :].astype(F32)
        cent = x - jnp.mean(x, axis=1, keepdims=True)
        rstd = lax.rsqrt(jnp.mean(cent * cent, axis=1, keepdims=True) + EPS)
        normed = cent * rstd
        nb[pl.ds(r, 64), :] = normed.astype(BF16)
        for j in range(HEADS):
            n8[j, pl.ds(r, 64), :] = normed[:, j * HD : (j + 1) * HD]
        rsd[pl.ds(r, 64), :] = jnp.broadcast_to(rstd, (64, HD))
        return carry

    loads[1].wait()
    lax.fori_loop(0, 2, norm_rows, 0)

    loads[0].wait()
    pl.semaphore_wait(barrier, HEADS - 1 + 3 + 2)
    greet(0, 1)
    fg_copies = [
        push(fg.at[0], fg.at[i], fg_s.at[i], fg_r.at[i], at_head(i)) for i in range(1, HEADS)
    ]
    for i in (6, 2, 7, 5, 3, 1, 4):
        fg_copies[i - 1].start()

    lax.fori_loop(2, 4, norm_rows, 0)
    pl.semaphore_wait(near.at[0], 2)
    greet(1, 2)

    loads[2].wait()
    for part in (3, 1, 2, 0):
        proj = nn(nb[...], wi[:, part * HD : (part + 1) * HD])
        sig = 0.5 * jnp.tanh(0.5 * proj) + 0.5
        act = (proj * sig).astype(BF16)
        slope[part] = sig * (1.0 + proj * (1.0 - sig))
        if part == 0:
            upart[...] = act.astype(F32)
        elif part == 1:
            kva[0, 1] = act
        elif part == 2:
            qa[0] = act
        else:
            kva[0, 0] = act
        if part == 1:
            kv_copies = [
                push(kva.at[0], kva.at[i], kv_s.at[i], kv_r.at[i], in_plane(i))
                for i in (3, 2, 1)
            ]
            for copy in kv_copies:
                copy.start()
        elif part == 2:
            pl.semaphore_wait(near.at[1], 2)
            greet(2, 4)
            q_copies = [
                push(qa.at[0], qa.at[d], q_s.at[d], q_r.at[d], at_z(PLANES - d))
                for d in range(REACH, 0, -1)
            ]
            for copy in q_copies:
                copy.start()

    loads[4].wait()
    attn = sa[...].astype(F32)
    cent = attn - jnp.mean(attn, axis=1, keepdims=True)
    arstd = lax.rsqrt(jnp.mean(cent * cent, axis=1, keepdims=True) + EPS)
    ahat_s[...] = cent * arstd
    arstd_s[...] = jnp.broadcast_to(arstd, (TOK, HD))
    kvg[...] = jnp.zeros_like(kvg)

    def turn_columns(j, carry):
        ntr[pl.ds(pl.multiple_of(j * HD, HD), HD), :] = n8[j].T.astype(BF16)
        return carry

    lax.fori_loop(0, HEADS, turn_columns, 0)

    loads[3].wait()
    dout = nn(fg[0], wo[pl.ds(pl.multiple_of(h * HD, HD), HD), :])
    for i in (1, 7, 4, 2, 6, 3, 5):
        fg_copies[i - 1].wait_recv()
        row = pl.multiple_of(((h + HEADS - i) % HEADS) * HD, HD)
        dout += nn(fg[i], wo[pl.ds(row, HD), :])
    ahat = ahat_s[...]
    dnorm = dout * upart[...]
    doa[0] = (
        (
            dnorm
            - jnp.mean(dnorm, axis=1, keepdims=True)
            - ahat * jnp.mean(dnorm * ahat, axis=1, keepdims=True)
        )
        * arstd_s[...]
    ).astype(BF16)
    do_copies = [
        push(doa.at[0], doa.at[d], do_s.at[d], do_r.at[d], at_z(PLANES - d))
        for d in range(REACH, 0, -1)
    ]
    for copy in do_copies:
        copy.start()

    dproj[:, 0:HD] = (dout * ahat * slope[0]).astype(BF16)
    gated = (ahat * upart[...]).astype(BF16)
    ge[:, :, :, 0:HD] = (nn(ntr[...], dproj[:, 0:HD])).astype(BF16).reshape(32, 2, 16, HD)

    def head_rows(i, carry):
        block = pl.ds(((h + HEADS - i) % HEADS) * 4, 4)
        ge[block, :, :, HD : 2 * HD] = tn(fg[i], gated).astype(BF16).reshape(4, 2, 16, HD)
        return carry

    lax.fori_loop(0, HEADS, head_rows, 0)

    def sum_parts(whole, into, over):
        return push(whole.at[:, 1 - c], into, over[0].at[0], over[1].at[0], in_plane(1))

    def add_first(whole, came, kept):
        def step(i, carry):
            kept[i] = (
                whole[pl.ds(2 * i, 2), c].astype(F32) + came[pl.ds(2 * i, 2)].astype(F32)
            ).astype(BF16)
            return carry

        lax.fori_loop(0, PLANES, step, 0)

    def sum_across(kept, into, over):
        return push(kept.at[:, 1 - xh], into, over[0].at[1], over[1].at[1], in_plane(2))

    def add_second(kept, came, final):
        def step(i, carry):
            final[i] = (kept[i, xh].astype(F32) + came[i].astype(F32)).astype(BF16)
            return carry

        lax.fori_loop(0, PLANES, step, 0)

    def sum_planes(final, into, over):
        return [
            push(final.at[(z + i) % PLANES], into.at[i], over[0].at[i], over[1].at[i], at_z(i))
            for i in NEAR_LAST
        ]

    def add_third(final, came):
        total = final[z].astype(F32)
        for i in range(1, PLANES):
            total += came[i].astype(F32)
        return total * GRAD_SCALE

    e_first = sum_parts(ge, ge1, (e12_s, e12_r))
    e_first.start()

    loads[5].wait()
    ends = []
    run = 0
    for i in range(NSEQ):
        run = run + lens[i]
        ends.append(run)
    own_plane = (z + PLANES // 2) % PLANES
    lane = lax.broadcasted_iota(jnp.int32, (1, TOK), 1)
    down = lax.broadcasted_iota(jnp.int32, (TOK, TOK), 0)

    def weigh(d):
        queries = qa[d]
        qpos = ((own_plane + d) % PLANES) * 1024 + xh * 512 + c * 256 + lane
        first = jnp.zeros((1, TOK), jnp.int32)
        for end in ends:
            first = jnp.maximum(first, jnp.where(qpos >= end, end, 0))

        def block(i, carry):
            base = own_plane * 1024 + ((xh + i // 2) % 2) * 512 + ((c + i) % 2) * 256
            mask = (down <= qpos - base) & (down >= first - base)
            scores = nt(kva[i, 0], queries) * SCALE
            sig = 0.5 * jnp.tanh(0.5 * scores) + 0.5
            weight = scores * sig
            slp[d, i] = jnp.where(mask, sig + weight * (1.0 - sig), 0.0)
            wts[d, i] = jnp.where(mask, weight, 0.0).astype(BF16)
            return carry

        lax.fori_loop(0, 4, block, 0)

    def gather_grads(d):
        queries = qa[d]
        upstream = doa[d]
        grad_q = jnp.zeros((HD, TOK), F32)
        for i in range(4):
            dscore = (nt(kva[i, 1], upstream) * slp[d, i]).astype(BF16)
            kvg[i, 0] += nn(dscore, queries)
            kvg[i, 1] += nn(wts[d, i], upstream)
            grad_q += nn(ktr[i], dscore)
        dqs[d] = grad_q.astype(BF16)

    for copy in kv_copies:
        copy.wait_recv()
    for i in range(4):
        ktr[i] = kva[i, 0].astype(F32).T.astype(BF16)
    weigh(0)

    e_first.wait_recv()
    add_first(ge, ge1, ga1)
    e_second = sum_across(ga1, ge2, (e12_s, e12_r))
    e_second.start()

    gather_grads(0)

    def weigh_step(turn, carry):
        d = REACH - turn
        push(qa.at[0], qa.at[d], q_s.at[d], q_r.at[d], at_z(d)).wait_recv()
        weigh(d)
        return carry

    lax.fori_loop(0, REACH, weigh_step, 0)

    e_second.wait_recv()
    add_second(ga1, ge2, ga2)
    pl.semaphore_wait(near.at[2], 2)

    def grads_step(turn, carry):
        d = REACH - turn
        push(doa.at[0], doa.at[d], do_s.at[d], do_r.at[d], at_z(d)).wait_recv()
        gather_grads(d)
        push(dqs.at[d], dqr.at[d], dq_s.at[d], dq_r.at[d], at_z(d)).start()
        return carry

    lax.fori_loop(0, REACH, grads_step, 0)

    for j in range(2):
        other = 2 * j + 1
        kvs1[j] = kvg[other].astype(BF16)
    k_first = push(kvs1, kvr1, kx_s.at[0], kx_r.at[0], in_plane(1))
    k_first.start()

    e_third = sum_planes(ga2, ge3, (e3_s, e3_r))
    for copy in e_third:
        copy.start()

    k_first.wait_recv()
    kvs2[...] = (kvg[2] + kvr1[1].astype(F32)).astype(BF16)
    k_second = push(kvs2, kvr2, kx_s.at[1], kx_r.at[1], in_plane(2))
    k_second.start()

    dq_copies = [
        push(dqs.at[d], dqr.at[d], dq_s.at[d], dq_r.at[d], at_z(d)) for d in range(1, REACH + 1)
    ]
    grad_q = dqs[0].astype(F32)
    for d in range(REACH, 0, -1):
        dq_copies[d - 1].wait_recv()
        grad_q += dqr[d].astype(F32)
    dproj[:, 2 * HD : 3 * HD] = (grad_q.T * (SCALE / MOST) * slope[2]).astype(BF16)
    gl[:, :, :, HD : 2 * HD] = (
        nn(ntr[...], dproj[:, 2 * HD : 3 * HD]).astype(BF16).reshape(32, 2, 16, HD)
    )

    k_second.wait_recv()
    grad_k = kvg[0, 0] + kvr1[0, 0].astype(F32) + kvr2[0].astype(F32)
    grad_v = kvg[0, 1] + kvr1[0, 1].astype(F32) + kvr2[1].astype(F32)
    dproj[:, 3 * HD :] = (grad_k * (SCALE / MOST) * slope[3]).astype(BF16)
    dproj[:, HD : 2 * HD] = (grad_v * (1.0 / MOST) * slope[1]).astype(BF16)
    gl[:, :, :, 2 * HD :] = nn(ntr[...], dproj[:, 3 * HD :]).astype(BF16).reshape(32, 2, 16, HD)
    gl[:, :, :, 0:HD] = nn(ntr[...], dproj[:, HD : 2 * HD]).astype(BF16).reshape(32, 2, 16, HD)
    l_first = sum_parts(gl, gl1, (l12_s, l12_r))
    l_first.start()

    total = jnp.zeros((TOK, HD), F32)
    along = jnp.zeros((TOK, HD), F32)
    p_copies = []

    def spread(i, total, along):
        hh = (h + i) % HEADS
        part = nt(dproj[...], wi[pl.ds(pl.multiple_of(hh * HD, HD), HD), :])
        if i:
            ps[i] = part.astype(BF16)
            copy = push(ps.at[i], pr.at[i], p_s.at[i], p_r.at[i], at_head(i))
            copy.start()
            p_copies.append((i, copy))
        else:
            own[...] = part
        return total + part, along + part * n8[hh]

    for i in (6, 2, 7):
        total, along = spread(i, total, along)

    l_first.wait_recv()
    add_first(gl, gl1, gb1)
    l_second = sum_across(gb1, gl2, (l12_s, l12_r))
    l_second.start()

    for i in (5, 3, 1, 4, 0):
        total, along = spread(i, total, along)
    lane = lax.broadcasted_iota(jnp.int32, (TOK, HD), 1)
    both = jnp.where(
        lane == 0,
        jnp.sum(total, axis=1, keepdims=True),
        jnp.where(lane == 1, jnp.sum(along, axis=1, keepdims=True), 0.0),
    )
    st[...] = both.T[0:8, :]
    t_copies = [
        push(st, sr.at[i], t_s.at[i], t_r.at[i], at_head(i)) for i in range(1, HEADS)
    ]
    for copy in t_copies:
        copy.start()

    for copy in e_third:
        copy.wait_recv()
    early = add_third(ga2, ge3)
    g1[:, 0:HD] = early[:, 0:HD]
    g2[...] = early[:, HD:]

    l_second.wait_recv()
    add_second(gb1, gl2, gb2)
    l_third = sum_planes(gb2, gl3, (l3_s, l3_r))
    for copy in l_third:
        copy.start()

    summed = own[...]
    for i, copy in p_copies:
        copy.wait_recv()
        summed += pr[i].astype(F32)
    stats = st[...]
    for i in range(1, HEADS):
        t_copies[i - 1].wait_recv()
        stats += sr[i]
    wide = jnp.concatenate([stats, jnp.zeros((HD - 8, TOK), F32)], axis=0).T * (1.0 / WIDTH)
    back = (summed - wide[:, 0:1] - n8[h] * wide[:, 1:2]) * rsd[...]
    gi[...] = (fg[0].astype(F32) + back).astype(BF16)

    for copy in (
        fg_copies + q_copies + kv_copies + do_copies + dq_copies + e_third + t_copies
    ):
        copy.wait_send()
    for i, copy in p_copies:
        copy.wait_send()
    for copy in (e_first, e_second, k_first, k_second, l_first, l_second):
        copy.wait_send()

    for copy in l_third:
        copy.wait_recv()
    late = add_third(gb2, gl3)
    g1[:, HD:] = late
    for copy in l_third:
        copy.wait_send()


def rows_of(columns):
    return [
        pltpu.VMEM((32, 2, 16, columns), BF16),
        pltpu.VMEM((32, 16, columns), BF16),
        pltpu.VMEM((16, 2, 16, columns), BF16),
        pltpu.VMEM((16, 16, columns), BF16),
        pltpu.VMEM((16, 16, columns), BF16),
        pltpu.VMEM((16, 16, columns), BF16),
    ]


def per_device(events, out_grad, saved_attn, in_weight, out_weight, lengths):
    tile = (TOK, HD)
    vmem = pl.BlockSpec(memory_space=pltpu.VMEM)
    dma = pltpu.SemaphoreType.DMA
    scratch = [
        pltpu.VMEM((TOK, WIDTH), BF16),
        pltpu.VMEM(tile, BF16),
        pltpu.VMEM((WIDTH, 4 * HD), BF16),
        pltpu.VMEM((WIDTH, HD), BF16),
        pltpu.SMEM((NSEQ,), jnp.int32),
        pltpu.VMEM((HEADS,) + tile, F32),
        pltpu.VMEM((TOK, WIDTH), BF16),
        pltpu.VMEM((WIDTH, TOK), BF16),
        pltpu.VMEM(tile, F32),
        pltpu.VMEM((4,) + tile, F32),
        pltpu.VMEM(tile, F32),
        pltpu.VMEM(tile, F32),
        pltpu.VMEM(tile, F32),
        pltpu.VMEM((TOK, 4 * HD), BF16),
        pltpu.VMEM((HEADS,) + tile, BF16),
        pltpu.VMEM((REACH + 1,) + tile, BF16),
        pltpu.VMEM((REACH + 1,) + tile, BF16),
        pltpu.VMEM((4, 2) + tile, BF16),
        pltpu.VMEM((4, HD, TOK), BF16),
        pltpu.VMEM((REACH + 1, 4, TOK, TOK), BF16),
        pltpu.VMEM((REACH + 1, 4, TOK, TOK), F32),
        pltpu.VMEM((4, 2) + tile, F32),
        pltpu.VMEM((REACH + 1, HD, TOK), BF16),
        pltpu.VMEM((REACH + 1, HD, TOK), BF16),
        pltpu.VMEM((2, 2) + tile, BF16),
        pltpu.VMEM((2, 2) + tile, BF16),
        pltpu.VMEM((2,) + tile, BF16),
        pltpu.VMEM((2,) + tile, BF16),
        *rows_of(2 * HD),
        *rows_of(3 * HD),
        pltpu.VMEM((HEADS,) + tile, BF16),
        pltpu.VMEM((HEADS,) + tile, BF16),
        pltpu.VMEM(tile, F32),
        pltpu.VMEM((8, TOK), F32),
        pltpu.VMEM((HEADS, 8, TOK), F32),
    ]
    counts = (8, 8, 5, 5, 5, 5, 4, 4, 5, 5, 2, 2, 2, 2, 16, 16, 2, 2, 16, 16, 8, 8, 8, 8)
    scratch += [dma((6,)), pltpu.SemaphoreType.REGULAR((3,))]
    scratch += [dma((n,)) for n in counts]
    return pl.pallas_call(
        kernel,
        out_shape=(
            jax.ShapeDtypeStruct(tile, BF16),
            jax.ShapeDtypeStruct((16, 4 * HD), F32),
            jax.ShapeDtypeStruct((16, HD), F32),
        ),
        in_specs=[pl.BlockSpec(memory_space=pl.ANY)] * 6,
        out_specs=(vmem,) * 3,
        scratch_shapes=scratch,
        compiler_params=pltpu.CompilerParams(
            collective_id=0, has_side_effects=True, vmem_limit_bytes=56 * 2**20
        ),
        name="layer_backward",
    )(events, out_grad, saved_attn, in_weight, out_weight, lengths)


def solution(mesh):
    return jax.shard_map(
        per_device,
        mesh=mesh,
        in_specs=(
            P("seq", None),
            P("seq", "head"),
            P("seq", "head"),
            P(None, "head"),
            P(None, "head"),
            P(),
        ),
        out_specs=(P("seq", "head"), P("seq", "head"), P("seq", "head")),
        check_vma=False,
    )
```

```python
import math

import jax
import jax.numpy as jnp
from jax import lax
from jax.experimental import pallas as pl
from jax.experimental.pallas import tpu as pltpu
from jax.sharding import PartitionSpec as P

HEADS = 8
HD = 128
TOK = 256
WIDTH = 1024
PLANES = 16
NSEQ = 16
REACH = 4
MOST = 4096.0
EPS = 1e-05
SCALE = 1.0 / math.sqrt(HD)
GRAD_SCALE = 1.0 / 128.0
MESH = pl.DeviceIdType.MESH
F32 = jnp.float32
BF16 = jnp.bfloat16
NEAR_LAST = (8, 7, 9, 6, 10, 5, 11, 4, 12, 3, 13, 2, 14, 1, 15)


def nn(a, b):
    return jnp.dot(a, b, preferred_element_type=F32)


def nt(a, b):
    return lax.dot_general(a, b, (((1,), (1,)), ((), ())), preferred_element_type=F32)


def tn(a, b):
    return lax.dot_general(a, b, (((0,), (0,)), ((), ())), preferred_element_type=F32)


def push(src, dst, sent, came, device):
    return pltpu.make_async_remote_copy(
        src_ref=src,
        dst_ref=dst,
        send_sem=sent,
        recv_sem=came,
        device_id=device,
        device_id_type=MESH,
    )


def kernel(
    ev_h, og_h, sa_h, wi_h, wo_h, lens_h, gi, g1, g2,
    ev, sa, wi, wo, lens,
    n8, nb, ntr, rsd, slope, rates, rates_in, upart, ahat_s, arstd_s, dproj,
    fg, qa, doa, kva, ktr, wts, slp, kvg, dqs, dqr,
    kvs1, kvr1, kvs2, kvr2,
    ge, ge1, ga1, ge2, ga2, ge3,
    gl, gl1, gb1, gl2, gb2, gl3,
    ps, pr, own, st, sr,
    in_s, near, x_s, x_r,
    fg_s, fg_r, q_s, q_r, do_s, do_r, kv_s, kv_r, dq_s, dq_r, kx_s, kx_r,
    e12_s, e12_r, e3_s, e3_r, l12_s, l12_r, l3_s, l3_r, p_s, p_r, t_s, t_r,
):
    s = lax.axis_index("seq")
    h = lax.axis_index("head")
    z = s // 4
    xh = (s // 2) % 2
    c = s % 2

    def at_z(i):
        return (((z + i) % PLANES) * 4 + xh * 2 + c, h)

    def in_plane(i):
        return (z * 4 + ((xh + i // 2) % 2) * 2 + (c + i % 2) % 2, h)

    def at_head(i):
        return (s, (h + i) % HEADS)

    barrier = pltpu.get_barrier_semaphore()
    for i in range(1, HEADS):
        pl.semaphore_signal(barrier, inc=1, device_id=at_head(i), device_id_type=MESH)
    for i in range(1, 4):
        pl.semaphore_signal(barrier, inc=1, device_id=in_plane(i), device_id_type=MESH)
    for i in (1, PLANES - 1):
        pl.semaphore_signal(barrier, inc=1, device_id=at_z(i), device_id_type=MESH)

    def greet(level, distance):
        for i in (distance, PLANES - distance):
            pl.semaphore_signal(
                near.at[level], inc=1, device_id=at_z(i), device_id_type=MESH
            )

    loads = [
        pltpu.make_async_copy(src, dst, in_s.at[i])
        for i, (src, dst) in enumerate(
            ((og_h, fg.at[0]), (ev_h, ev), (wi_h, wi), (wo_h, wo), (sa_h, sa), (lens_h, lens))
        )
    ]
    for copy in loads:
        copy.start()

    def norm_rows(i, carry):
        r = pl.multiple_of(i * 64, 64)
        x = ev[pl.ds(r, 64), :].astype(F32)
        cent = x - jnp.mean(x, axis=1, keepdims=True)
        rstd = lax.rsqrt(jnp.mean(cent * cent, axis=1, keepdims=True) + EPS)
        normed = cent * rstd
        nb[pl.ds(r, 64), :] = normed.astype(BF16)
        for j in range(HEADS):
            n8[j, pl.ds(r, 64), :] = normed[:, j * HD : (j + 1) * HD]
        rsd[pl.ds(r, 64), :] = jnp.broadcast_to(rstd, (64, HD))
        return carry

    loads[1].wait()
    lax.fori_loop(0, 2, norm_rows, 0)

    loads[0].wait()
    pl.semaphore_wait(barrier, HEADS - 1 + 3 + 2)
    greet(0, 1)
    fg_copies = [
        push(fg.at[0], fg.at[i], fg_s.at[i], fg_r.at[i], at_head(i)) for i in range(1, HEADS)
    ]
    for i in (6, 2, 7, 5, 3, 1, 4):
        fg_copies[i - 1].start()

    lax.fori_loop(2, 4, norm_rows, 0)
    pl.semaphore_wait(near.at[0], 2)
    greet(1, 2)

    def hop_queries(d):
        return push(qa.at[d], qa.at[d + 1], q_s.at[d], q_r.at[d + 1], at_z(PLANES - 1))

    loads[2].wait()
    for part in (3, 1, 2, 0):
        proj = nn(nb[...], wi[:, part * HD : (part + 1) * HD])
        sig = 0.5 * jnp.tanh(0.5 * proj) + 0.5
        act = (proj * sig).astype(BF16)
        rate = sig * (1.0 + proj * (1.0 - sig))
        slope[part] = rate
        if part in (1, 3):
            rates[part // 2] = rate.astype(BF16)
        if part == 0:
            upart[...] = act.astype(F32)
        elif part == 1:
            kva[0, 1] = act
        elif part == 2:
            qa[0] = act
        else:
            kva[0, 0] = act
        if part == 1:
            kv_copies = [
                push(kva.at[0], kva.at[i], kv_s.at[i], kv_r.at[i], in_plane(i))
                for i in (3, 2, 1)
            ]
            for copy in kv_copies:
                copy.start()
        elif part == 2:
            hop_queries(0).start()

    loads[4].wait()
    attn = sa[...].astype(F32)
    cent = attn - jnp.mean(attn, axis=1, keepdims=True)
    arstd = lax.rsqrt(jnp.mean(cent * cent, axis=1, keepdims=True) + EPS)
    ahat_s[...] = cent * arstd
    arstd_s[...] = jnp.broadcast_to(arstd, (TOK, HD))
    pl.semaphore_wait(near.at[1], 2)
    greet(2, 4)

    loads[3].wait()
    dout = nn(fg[0], wo[pl.ds(pl.multiple_of(h * HD, HD), HD), :])
    for i in (1, 7, 4, 2, 6, 3, 5):
        fg_copies[i - 1].wait_recv()
        row = pl.multiple_of(((h + HEADS - i) % HEADS) * HD, HD)
        dout += nn(fg[i], wo[pl.ds(row, HD), :])
    ahat = ahat_s[...]
    dnorm = dout * upart[...]
    doa[0] = (
        (
            dnorm
            - jnp.mean(dnorm, axis=1, keepdims=True)
            - ahat * jnp.mean(dnorm * ahat, axis=1, keepdims=True)
        )
        * arstd_s[...]
    ).astype(BF16)
    do_copies = [
        push(doa.at[0], doa.at[d], do_s.at[d], do_r.at[d], at_z(PLANES - d))
        for d in range(REACH, 0, -1)
    ]
    for copy in do_copies:
        copy.start()
    hop_queries(0).wait_recv()
    hop_queries(1).start()

    def turn_columns(j, carry):
        ntr[0, pl.ds(pl.multiple_of(j * HD, HD), HD), :] = n8[j].T.astype(BF16)
        return carry

    lax.fori_loop(0, HEADS, turn_columns, 0)
    kvg[...] = jnp.zeros_like(kvg)
    x_copies = [
        push(ntr.at[0], ntr.at[1], x_s.at[0], x_r.at[0], in_plane(2)),
        push(rates, rates_in, x_s.at[1], x_r.at[1], in_plane(2)),
    ]
    for copy in x_copies:
        copy.start()

    dproj[:, 0:HD] = (dout * ahat * slope[0]).astype(BF16)
    gated = (ahat * upart[...]).astype(BF16)
    ge[:, :, :, 0:HD] = (nn(ntr[0], dproj[:, 0:HD])).astype(BF16).reshape(32, 2, 16, HD)

    def head_rows(i, carry):
        block = pl.ds(((h + HEADS - i) % HEADS) * 4, 4)
        ge[block, :, :, HD : 2 * HD] = tn(fg[i], gated).astype(BF16).reshape(4, 2, 16, HD)
        return carry

    lax.fori_loop(0, HEADS, head_rows, 0)

    def sum_parts(whole, into, over):
        return push(whole.at[:, 1 - c], into, over[0].at[0], over[1].at[0], in_plane(1))

    def add_first(whole, came, kept):
        def step(i, carry):
            kept[i] = (
                whole[pl.ds(2 * i, 2), c].astype(F32) + came[pl.ds(2 * i, 2)].astype(F32)
            ).astype(BF16)
            return carry

        lax.fori_loop(0, PLANES, step, 0)

    def sum_across(kept, into, over):
        return push(kept.at[:, 1 - xh], into, over[0].at[1], over[1].at[1], in_plane(2))

    def add_second(kept, came, final):
        def step(i, carry):
            final[i] = (kept[i, xh].astype(F32) + came[i].astype(F32)).astype(BF16)
            return carry

        lax.fori_loop(0, PLANES, step, 0)

    def sum_planes(final, into, over):
        return [
            push(final.at[(z + i) % PLANES], into.at[i], over[0].at[i], over[1].at[i], at_z(i))
            for i in NEAR_LAST
        ]

    def add_third(final, came):
        total = final[z].astype(F32)
        for i in range(1, PLANES):
            total += came[i].astype(F32)
        return total * GRAD_SCALE

    e_first = sum_parts(ge, ge1, (e12_s, e12_r))
    e_first.start()

    loads[5].wait()
    ends = []
    run = 0
    for i in range(NSEQ):
        run = run + lens[i]
        ends.append(run)
    own_plane = (z + PLANES // 2) % PLANES
    lane = lax.broadcasted_iota(jnp.int32, (1, TOK), 1)
    down = lax.broadcasted_iota(jnp.int32, (TOK, TOK), 0)

    def weigh(d):
        queries = qa[d]
        qpos = ((own_plane + d) % PLANES) * 1024 + xh * 512 + c * 256 + lane
        first = jnp.zeros((1, TOK), jnp.int32)
        for end in ends:
            first = jnp.maximum(first, jnp.where(qpos >= end, end, 0))

        def block(i, carry):
            base = own_plane * 1024 + ((xh + i // 2) % 2) * 512 + ((c + i) % 2) * 256
            mask = (down <= qpos - base) & (down >= first - base)
            scores = nt(kva[i, 0], queries) * SCALE
            sig = 0.5 * jnp.tanh(0.5 * scores) + 0.5
            weight = scores * sig
            slp[d, i] = jnp.where(mask, sig + weight * (1.0 - sig), 0.0)
            wts[d, i] = jnp.where(mask, weight, 0.0).astype(BF16)
            return carry

        lax.fori_loop(0, 4, block, 0)

    def gather_grads(d):
        queries = qa[d]
        upstream = doa[d]
        grad_q = jnp.zeros((HD, TOK), F32)
        for i in range(4):
            dscore = (nt(kva[i, 1], upstream) * slp[d, i]).astype(BF16)
            kvg[i, 0] += nn(dscore, queries)
            kvg[i, 1] += nn(wts[d, i], upstream)
            grad_q += nn(ktr[i], dscore)
        dqs[d] = grad_q.astype(BF16)

    for copy in kv_copies:
        copy.wait_recv()
    for i in range(4):
        ktr[i] = kva[i, 0].astype(F32).T.astype(BF16)
    weigh(0)
    hop_queries(1).wait_recv()
    hop_queries(2).start()

    e_first.wait_recv()
    add_first(ge, ge1, ga1)
    e_second = sum_across(ga1, ge2, (e12_s, e12_r))
    e_second.start()

    gather_grads(0)

    def weigh_step(turn, carry):
        d = turn + 1

        @pl.when(d == REACH - 1)
        def _():
            hop_queries(2).wait_recv()
            hop_queries(3).start()

        @pl.when(d == REACH)
        def _():
            hop_queries(3).wait_recv()

        weigh(d)
        return carry

    lax.fori_loop(0, REACH, weigh_step, 0)

    e_second.wait_recv()
    add_second(ga1, ge2, ga2)
    pl.semaphore_wait(near.at[2], 2)

    def grads_step(turn, carry):
        d = REACH - turn
        push(doa.at[0], doa.at[d], do_s.at[d], do_r.at[d], at_z(d)).wait_recv()
        gather_grads(d)
        push(dqs.at[d], dqr.at[d], dq_s.at[d], dq_r.at[d], at_z(d)).start()
        return carry

    lax.fori_loop(0, REACH, grads_step, 0)

    for j in range(2):
        other = 2 * j + 1
        kvs1[j] = kvg[other].astype(BF16)
    k_first = push(kvs1, kvr1, kx_s.at[0], kx_r.at[0], in_plane(1))
    k_first.start()

    e_third = sum_planes(ga2, ge3, (e3_s, e3_r))
    for copy in e_third:
        copy.start()

    for copy in x_copies:
        copy.wait_recv()
    k_first.wait_recv()
    mine = kvg[0] + kvr1[0].astype(F32)
    other = kvg[2] + kvr1[1].astype(F32)
    kvs2[...] = other.astype(BF16)
    k_second = push(kvs2, kvr2, kx_s.at[1], kx_r.at[1], in_plane(2))
    k_second.start()
    key_scale = SCALE / MOST
    value_scale = 1.0 / MOST
    here = jnp.concatenate(
        [mine[1] * value_scale * slope[1], mine[0] * key_scale * slope[3]], axis=1
    ).astype(BF16)
    there = jnp.concatenate(
        [
            other[1] * value_scale * rates_in[0].astype(F32),
            other[0] * key_scale * rates_in[1].astype(F32),
        ],
        axis=1,
    ).astype(BF16)
    gl[:, :, :, 0 : 2 * HD] = (
        (nn(ntr[0], here) + nn(ntr[1], there)).astype(BF16).reshape(32, 2, 16, 2 * HD)
    )

    dq_copies = [
        push(dqs.at[d], dqr.at[d], dq_s.at[d], dq_r.at[d], at_z(d)) for d in range(1, REACH + 1)
    ]
    grad_q = dqs[0].astype(F32)
    for d in range(REACH, 0, -1):
        dq_copies[d - 1].wait_recv()
        grad_q += dqr[d].astype(F32)
    dproj[:, 2 * HD : 3 * HD] = (grad_q.T * key_scale * slope[2]).astype(BF16)
    gl[:, :, :, 2 * HD :] = (
        nn(ntr[0], dproj[:, 2 * HD : 3 * HD]).astype(BF16).reshape(32, 2, 16, HD)
    )
    l_first = sum_parts(gl, gl1, (l12_s, l12_r))
    l_first.start()
    l_first.wait_recv()
    add_first(gl, gl1, gb1)
    l_second = sum_across(gb1, gl2, (l12_s, l12_r))
    l_second.start()

    k_second.wait_recv()
    grad_k = mine[0] + kvr2[0].astype(F32)
    grad_v = mine[1] + kvr2[1].astype(F32)
    dproj[:, 3 * HD :] = (grad_k * key_scale * slope[3]).astype(BF16)
    dproj[:, HD : 2 * HD] = (grad_v * value_scale * slope[1]).astype(BF16)

    total = jnp.zeros((TOK, HD), F32)
    along = jnp.zeros((TOK, HD), F32)
    p_copies = []

    def spread(i, total, along):
        hh = (h + i) % HEADS
        part = nt(dproj[...], wi[pl.ds(pl.multiple_of(hh * HD, HD), HD), :])
        if i:
            ps[i] = part.astype(BF16)
            copy = push(ps.at[i], pr.at[i], p_s.at[i], p_r.at[i], at_head(i))
            copy.start()
            p_copies.append((i, copy))
        else:
            own[...] = part
        return total + part, along + part * n8[hh]

    for i in (6, 2, 7, 5, 3, 1, 4, 0):
        total, along = spread(i, total, along)
    lane = lax.broadcasted_iota(jnp.int32, (TOK, HD), 1)
    both = jnp.where(
        lane == 0,
        jnp.sum(total, axis=1, keepdims=True),
        jnp.where(lane == 1, jnp.sum(along, axis=1, keepdims=True), 0.0),
    )
    st[...] = both.T[0:8, :]
    t_copies = [
        push(st, sr.at[i], t_s.at[i], t_r.at[i], at_head(i)) for i in range(1, HEADS)
    ]
    for copy in t_copies:
        copy.start()

    for copy in e_third:
        copy.wait_recv()
    early = add_third(ga2, ge3)
    g1[:, 0:HD] = early[:, 0:HD]
    g2[...] = early[:, HD:]

    l_second.wait_recv()
    add_second(gb1, gl2, gb2)
    l_third = sum_planes(gb2, gl3, (l3_s, l3_r))
    for copy in l_third:
        copy.start()

    summed = own[...]
    for i, copy in p_copies:
        copy.wait_recv()
        summed += pr[i].astype(F32)
    stats = st[...]
    for i in range(1, HEADS):
        t_copies[i - 1].wait_recv()
        stats += sr[i]
    wide = jnp.concatenate([stats, jnp.zeros((HD - 8, TOK), F32)], axis=0).T * (1.0 / WIDTH)
    back = (summed - wide[:, 0:1] - n8[h] * wide[:, 1:2]) * rsd[...]
    gi[...] = (fg[0].astype(F32) + back).astype(BF16)

    for copy in (
        fg_copies + kv_copies + do_copies + dq_copies + e_third + t_copies + x_copies
    ):
        copy.wait_send()
    for d in range(REACH):
        hop_queries(d).wait_send()
    for i, copy in p_copies:
        copy.wait_send()
    for copy in (e_first, e_second, k_first, k_second, l_first, l_second):
        copy.wait_send()

    for copy in l_third:
        copy.wait_recv()
    late = add_third(gb2, gl3)
    g1[:, HD : 2 * HD] = late[:, 0:HD]
    g1[:, 2 * HD : 3 * HD] = late[:, 2 * HD :]
    g1[:, 3 * HD :] = late[:, HD : 2 * HD]
    for copy in l_third:
        copy.wait_send()


def rows_of(columns):
    return [
        pltpu.VMEM((32, 2, 16, columns), BF16),
        pltpu.VMEM((32, 16, columns), BF16),
        pltpu.VMEM((16, 2, 16, columns), BF16),
        pltpu.VMEM((16, 16, columns), BF16),
        pltpu.VMEM((16, 16, columns), BF16),
        pltpu.VMEM((16, 16, columns), BF16),
    ]


def per_device(events, out_grad, saved_attn, in_weight, out_weight, lengths):
    tile = (TOK, HD)
    vmem = pl.BlockSpec(memory_space=pltpu.VMEM)
    dma = pltpu.SemaphoreType.DMA
    scratch = [
        pltpu.VMEM((TOK, WIDTH), BF16),
        pltpu.VMEM(tile, BF16),
        pltpu.VMEM((WIDTH, 4 * HD), BF16),
        pltpu.VMEM((WIDTH, HD), BF16),
        pltpu.SMEM((NSEQ,), jnp.int32),
        pltpu.VMEM((HEADS,) + tile, F32),
        pltpu.VMEM((TOK, WIDTH), BF16),
        pltpu.VMEM((2, WIDTH, TOK), BF16),
        pltpu.VMEM(tile, F32),
        pltpu.VMEM((4,) + tile, F32),
        pltpu.VMEM((2,) + tile, BF16),
        pltpu.VMEM((2,) + tile, BF16),
        pltpu.VMEM(tile, F32),
        pltpu.VMEM(tile, F32),
        pltpu.VMEM(tile, F32),
        pltpu.VMEM((TOK, 4 * HD), BF16),
        pltpu.VMEM((HEADS,) + tile, BF16),
        pltpu.VMEM((REACH + 1,) + tile, BF16),
        pltpu.VMEM((REACH + 1,) + tile, BF16),
        pltpu.VMEM((4, 2) + tile, BF16),
        pltpu.VMEM((4, HD, TOK), BF16),
        pltpu.VMEM((REACH + 1, 4, TOK, TOK), BF16),
        pltpu.VMEM((REACH + 1, 4, TOK, TOK), F32),
        pltpu.VMEM((4, 2) + tile, F32),
        pltpu.VMEM((REACH + 1, HD, TOK), BF16),
        pltpu.VMEM((REACH + 1, HD, TOK), BF16),
        pltpu.VMEM((2, 2) + tile, BF16),
        pltpu.VMEM((2, 2) + tile, BF16),
        pltpu.VMEM((2,) + tile, BF16),
        pltpu.VMEM((2,) + tile, BF16),
        *rows_of(2 * HD),
        *rows_of(3 * HD),
        pltpu.VMEM((HEADS,) + tile, BF16),
        pltpu.VMEM((HEADS,) + tile, BF16),
        pltpu.VMEM(tile, F32),
        pltpu.VMEM((8, TOK), F32),
        pltpu.VMEM((HEADS, 8, TOK), F32),
    ]
    counts = (8, 8, 5, 5, 5, 5, 4, 4, 5, 5, 2, 2, 2, 2, 16, 16, 2, 2, 16, 16, 8, 8, 8, 8)
    scratch += [dma((6,)), pltpu.SemaphoreType.REGULAR((3,)), dma((2,)), dma((2,))]
    scratch += [dma((n,)) for n in counts]
    return pl.pallas_call(
        kernel,
        out_shape=(
            jax.ShapeDtypeStruct(tile, BF16),
            jax.ShapeDtypeStruct((16, 4 * HD), F32),
            jax.ShapeDtypeStruct((16, HD), F32),
        ),
        in_specs=[pl.BlockSpec(memory_space=pl.ANY)] * 6,
        out_specs=(vmem,) * 3,
        scratch_shapes=scratch,
        compiler_params=pltpu.CompilerParams(
            collective_id=0, has_side_effects=True, vmem_limit_bytes=56 * 2**20
        ),
        name="layer_backward",
    )(events, out_grad, saved_attn, in_weight, out_weight, lengths)


def solution(mesh):
    return jax.shard_map(
        per_device,
        mesh=mesh,
        in_specs=(
            P("seq", None),
            P("seq", "head"),
            P("seq", "head"),
            P(None, "head"),
            P(None, "head"),
            P(),
        ),
        out_specs=(P("seq", "head"), P("seq", "head"), P("seq", "head")),
        check_vma=False,
    )
```

```python
import math

import jax
import jax.numpy as jnp
from jax import lax
from jax.experimental import pallas as pl
from jax.experimental.pallas import tpu as pltpu
from jax.sharding import PartitionSpec as P

HEADS = 8
HD = 128
TOK = 256
WIDTH = 1024
PLANES = 16
NSEQ = 16
REACH = 4
MOST = 4096.0
EPS = 1e-05
SCALE = 1.0 / math.sqrt(HD)
GRAD_SCALE = 1.0 / 128.0
MESH = pl.DeviceIdType.MESH
F32 = jnp.float32
BF16 = jnp.bfloat16
NEAR_LAST = (8, 7, 9, 6, 10, 5, 11, 4, 12, 3, 13, 2, 14, 1, 15)


def nn(a, b):
    return jnp.dot(a, b, preferred_element_type=F32)


def nt(a, b):
    return lax.dot_general(a, b, (((1,), (1,)), ((), ())), preferred_element_type=F32)


def tn(a, b):
    return lax.dot_general(a, b, (((0,), (0,)), ((), ())), preferred_element_type=F32)


def push(src, dst, sent, came, device):
    return pltpu.make_async_remote_copy(
        src_ref=src,
        dst_ref=dst,
        send_sem=sent,
        recv_sem=came,
        device_id=device,
        device_id_type=MESH,
    )


def kernel(
    ev_h, og_h, sa_h, wi_h, wo_h, lens_h, gi, g1, g2,
    ev, sa, wi, wo, lens,
    n8, nb, ntr, rsd, slope, upart, ahat_s, arstd_s, dproj,
    fg, qa, doa, kva, ktr, begin, rowpos, kvg, dqs, dqr,
    kvs1, kvr1, kvs2, kvr2,
    ge, ge1, ga1, ge2, ga2, ge3,
    gl, gl1, gb1, gl2, gb2, gl3,
    ps, pr, own, st, sr,
    in_s, near,
    fg_s, fg_r, q_s, q_r, do_s, do_r, kv_s, kv_r, dq_s, dq_r, kx_s, kx_r,
    e12_s, e12_r, e3_s, e3_r, l12_s, l12_r, l3_s, l3_r, p_s, p_r, t_s, t_r,
):
    s = lax.axis_index("seq")
    h = lax.axis_index("head")
    z = s // 4
    xh = (s // 2) % 2
    c = s % 2

    def at_z(i):
        return (((z + i) % PLANES) * 4 + xh * 2 + c, h)

    def in_plane(i):
        return (z * 4 + ((xh + i // 2) % 2) * 2 + (c + i % 2) % 2, h)

    def at_head(i):
        return (s, (h + i) % HEADS)

    barrier = pltpu.get_barrier_semaphore()
    for i in range(1, HEADS):
        pl.semaphore_signal(barrier, inc=1, device_id=at_head(i), device_id_type=MESH)
    for i in range(1, 4):
        pl.semaphore_signal(barrier, inc=1, device_id=in_plane(i), device_id_type=MESH)
    for i in (1, PLANES - 1):
        pl.semaphore_signal(barrier, inc=1, device_id=at_z(i), device_id_type=MESH)

    def greet(level, distance):
        for i in (distance, PLANES - distance):
            pl.semaphore_signal(
                near.at[level], inc=1, device_id=at_z(i), device_id_type=MESH
            )

    loads = [
        pltpu.make_async_copy(src, dst, in_s.at[i])
        for i, (src, dst) in enumerate(
            ((og_h, fg.at[0]), (ev_h, ev), (wi_h, wi), (wo_h, wo), (sa_h, sa), (lens_h, lens))
        )
    ]
    for copy in loads:
        copy.start()

    def norm_rows(i, carry):
        r = pl.multiple_of(i * 64, 64)
        x = ev[pl.ds(r, 64), :].astype(F32)
        cent = x - jnp.mean(x, axis=1, keepdims=True)
        rstd = lax.rsqrt(jnp.mean(cent * cent, axis=1, keepdims=True) + EPS)
        normed = cent * rstd
        nb[pl.ds(r, 64), :] = normed.astype(BF16)
        for j in range(HEADS):
            n8[j, pl.ds(r, 64), :] = normed[:, j * HD : (j + 1) * HD]
        rsd[pl.ds(r, 64), :] = jnp.broadcast_to(rstd, (64, HD))
        return carry

    loads[1].wait()
    lax.fori_loop(0, 2, norm_rows, 0)

    loads[0].wait()
    pl.semaphore_wait(barrier, HEADS - 1 + 3 + 2)
    greet(0, 1)
    fg_copies = [
        push(fg.at[0], fg.at[i], fg_s.at[i], fg_r.at[i], at_head(i)) for i in range(1, HEADS)
    ]
    for i in (6, 2, 7, 5, 3, 1, 4):
        fg_copies[i - 1].start()

    lax.fori_loop(2, 4, norm_rows, 0)
    pl.semaphore_wait(near.at[0], 2)
    greet(1, 2)

    def hop_queries(d):
        return push(qa.at[d], qa.at[d + 1], q_s.at[d], q_r.at[d + 1], at_z(PLANES - 1))

    loads[2].wait()
    for part in (3, 1, 2, 0):
        proj = nn(nb[...], wi[:, part * HD : (part + 1) * HD])
        sig = 0.5 * jnp.tanh(0.5 * proj) + 0.5
        act = (proj * sig).astype(BF16)
        slope[part] = sig * (1.0 + proj * (1.0 - sig))
        if part == 0:
            upart[...] = act.astype(F32)
        elif part == 1:
            kva[0, 1] = act
        elif part == 2:
            qa[0] = act
        else:
            kva[0, 0] = act
        if part == 1:
            kv_copies = [
                push(kva.at[0], kva.at[i], kv_s.at[i], kv_r.at[i], in_plane(i))
                for i in (3, 2, 1)
            ]
            for copy in kv_copies:
                copy.start()
        elif part == 2:
            hop_queries(0).start()

    loads[4].wait()
    attn = sa[...].astype(F32)
    cent = attn - jnp.mean(attn, axis=1, keepdims=True)
    arstd = lax.rsqrt(jnp.mean(cent * cent, axis=1, keepdims=True) + EPS)
    ahat_s[...] = cent * arstd
    arstd_s[...] = jnp.broadcast_to(arstd, (TOK, HD))
    pl.semaphore_wait(near.at[1], 2)
    greet(2, 4)

    loads[3].wait()
    dout = nn(fg[0], wo[pl.ds(pl.multiple_of(h * HD, HD), HD), :])
    for i in (1, 7, 4, 2, 6, 3, 5):
        fg_copies[i - 1].wait_recv()
        row = pl.multiple_of(((h + HEADS - i) % HEADS) * HD, HD)
        dout += nn(fg[i], wo[pl.ds(row, HD), :])
    ahat = ahat_s[...]
    dnorm = dout * upart[...]
    doa[0] = (
        (
            dnorm
            - jnp.mean(dnorm, axis=1, keepdims=True)
            - ahat * jnp.mean(dnorm * ahat, axis=1, keepdims=True)
        )
        * arstd_s[...]
    ).astype(BF16)
    do_copies = [
        push(doa.at[0], doa.at[d], do_s.at[d], do_r.at[d], at_z(PLANES - d))
        for d in (2, 4, 3, 1)
    ]
    for copy in do_copies:
        copy.start()
    hop_queries(0).wait_recv()
    hop_queries(1).start()

    def turn_columns(j, carry):
        ntr[pl.ds(pl.multiple_of(j * HD, HD), HD), :] = n8[j].T.astype(BF16)
        return carry

    lax.fori_loop(0, HEADS, turn_columns, 0)

    dproj[:, 0:HD] = (dout * ahat * slope[0]).astype(BF16)
    gated = (ahat * upart[...]).astype(BF16)
    ge[:, :, :, 0:HD] = (nn(ntr[...], dproj[:, 0:HD])).astype(BF16).reshape(32, 2, 16, HD)

    def head_rows(i, carry):
        block = pl.ds(((h + HEADS - i) % HEADS) * 4, 4)
        ge[block, :, :, HD : 2 * HD] = tn(fg[i], gated).astype(BF16).reshape(4, 2, 16, HD)
        return carry

    lax.fori_loop(0, HEADS, head_rows, 0)

    def sum_parts(whole, into, over):
        return push(whole.at[:, 1 - c], into, over[0].at[0], over[1].at[0], in_plane(1))

    def add_first(whole, came, kept):
        def step(i, carry):
            kept[i] = (
                whole[pl.ds(2 * i, 2), c].astype(F32) + came[pl.ds(2 * i, 2)].astype(F32)
            ).astype(BF16)
            return carry

        lax.fori_loop(0, PLANES, step, 0)

    def sum_across(kept, into, over):
        return push(kept.at[:, 1 - xh], into, over[0].at[1], over[1].at[1], in_plane(2))

    def add_second(kept, came, final):
        def step(i, carry):
            final[i] = (kept[i, xh].astype(F32) + came[i].astype(F32)).astype(BF16)
            return carry

        lax.fori_loop(0, PLANES, step, 0)

    def sum_planes(final, into, over):
        return [
            push(final.at[(z + i) % PLANES], into.at[i], over[0].at[i], over[1].at[i], at_z(i))
            for i in NEAR_LAST
        ]

    def add_third(final, came):
        total = final[z].astype(F32)
        for i in range(1, PLANES):
            total += came[i].astype(F32)
        return total * GRAD_SCALE

    e_first = sum_parts(ge, ge1, (e12_s, e12_r))
    e_first.start()

    hop_queries(1).wait_recv()
    hop_queries(2).start()

    loads[5].wait()
    ends = []
    run = 0
    for i in range(NSEQ):
        run = run + lens[i]
        ends.append(run)
    own_plane = (z + PLANES // 2) % PLANES

    def history_starts(d, carry):
        plane = own_plane + d
        qpos = plane * 1024 + xh * 512 + c * 256 + lax.broadcasted_iota(jnp.int32, (8, TOK), 1)
        first = jnp.zeros((8, TOK), jnp.int32)
        for end in ends:
            first = jnp.maximum(first, jnp.where(qpos >= end, end, 0))
        begin[d] = jnp.where(plane < PLANES, first - own_plane * 1024, 2 * 1024)
        return carry

    lax.fori_loop(0, REACH + 1, history_starts, 0)

    for copy in kv_copies:
        copy.wait_recv()
    for i in range(4):
        ktr[:, i * TOK : (i + 1) * TOK] = kva[i, 0].astype(F32).T.astype(BF16)

    def slot_rows(shape):
        row = lax.broadcasted_iota(jnp.int32, shape, 0)
        half = row // 512
        quarter = (row // 256) % 2
        place = jnp.where(xh == 0, half, 1 - half) * 512
        place += jnp.where(c == 0, quarter, 1 - quarter) * 256
        return place + row % 256

    rowpos[...] = slot_rows((4 * TOK, HD))

    def attend(d, same):
        queries = qa[d]
        upstream = doa[d]
        keys = kva[:, 0].reshape(4 * TOK, HD)
        values = kva[:, 1].reshape(4 * TOK, HD)
        down = jnp.concatenate([rowpos[...]] * 2, axis=1)
        mask = down >= begin[d, 0:1, :]
        if same:
            lane = lax.broadcasted_iota(jnp.int32, (1, TOK), 1)
            mask = mask & (down <= xh * 512 + c * 256 + lane)
        half = nt(keys, queries) * (0.5 * SCALE)
        bell = 1.0 + jnp.tanh(half)
        weight = half * bell
        sig = 0.5 * bell
        dprob = nt(values, upstream)
        dscore = jnp.where(mask, dprob * (sig + weight * (1.0 - sig)), 0.0).astype(BF16)
        weight = jnp.where(mask, weight, 0.0).astype(BF16)
        grad_k = nn(dscore, queries).reshape(4, TOK, HD)
        grad_v = nn(weight, upstream).reshape(4, TOK, HD)
        if same:
            kvg[:, 0] = grad_k
            kvg[:, 1] = grad_v
        else:
            kvg[:, 0] += grad_k
            kvg[:, 1] += grad_v
        dqs[d] = nn(ktr[...], dscore).astype(BF16)

    attend(0, True)

    e_first.wait_recv()
    add_first(ge, ge1, ga1)
    e_second = sum_across(ga1, ge2, (e12_s, e12_r))
    e_second.start()

    hop_queries(2).wait_recv()
    hop_queries(3).start()

    def attend_step(turn, carry):
        d = jnp.where(turn == 0, 2, jnp.where(turn == 1, 1, turn + 1))

        @pl.when(d == REACH)
        def _():
            hop_queries(3).wait_recv()

        push(doa.at[0], doa.at[d], do_s.at[d], do_r.at[d], at_z(d)).wait_recv()
        attend(d, False)
        push(dqs.at[d], dqr.at[d], dq_s.at[d], dq_r.at[d], at_z(d)).start()
        return carry

    lax.fori_loop(0, REACH, attend_step, 0)

    for j in range(2):
        other = 2 * j + 1
        kvs1[j] = kvg[other].astype(BF16)
    k_first = push(kvs1, kvr1, kx_s.at[0], kx_r.at[0], in_plane(1))
    k_first.start()

    e_second.wait_recv()
    add_second(ga1, ge2, ga2)
    pl.semaphore_wait(near.at[2], 2)
    e_third = sum_planes(ga2, ge3, (e3_s, e3_r))
    for copy in e_third:
        copy.start()

    k_first.wait_recv()
    kvs2[...] = (kvg[2] + kvr1[1].astype(F32)).astype(BF16)
    k_second = push(kvs2, kvr2, kx_s.at[1], kx_r.at[1], in_plane(2))
    k_second.start()

    dq_copies = [
        push(dqs.at[d], dqr.at[d], dq_s.at[d], dq_r.at[d], at_z(d)) for d in range(1, REACH + 1)
    ]
    grad_q = dqs[0].astype(F32)
    for d in range(REACH, 0, -1):
        dq_copies[d - 1].wait_recv()
        grad_q += dqr[d].astype(F32)
    dproj[:, 2 * HD : 3 * HD] = (grad_q.T * (SCALE / MOST) * slope[2]).astype(BF16)
    gl[:, :, :, 2 * HD :] = (
        nn(ntr[...], dproj[:, 2 * HD : 3 * HD]).astype(BF16).reshape(32, 2, 16, HD)
    )

    k_second.wait_recv()
    grad_k = kvg[0, 0] + kvr1[0, 0].astype(F32) + kvr2[0].astype(F32)
    grad_v = kvg[0, 1] + kvr1[0, 1].astype(F32) + kvr2[1].astype(F32)
    dproj[:, 3 * HD :] = (grad_k * (SCALE / MOST) * slope[3]).astype(BF16)
    dproj[:, HD : 2 * HD] = (grad_v * (1.0 / MOST) * slope[1]).astype(BF16)
    pair = jnp.concatenate([dproj[:, HD : 2 * HD], dproj[:, 3 * HD :]], axis=1)
    gl[:, :, :, 0 : 2 * HD] = nn(ntr[...], pair).astype(BF16).reshape(32, 2, 16, 2 * HD)
    l_first = sum_parts(gl, gl1, (l12_s, l12_r))
    l_first.start()
    l_first.wait_recv()
    add_first(gl, gl1, gb1)
    l_second = sum_across(gb1, gl2, (l12_s, l12_r))
    l_second.start()

    total = jnp.zeros((TOK, HD), F32)
    along = jnp.zeros((TOK, HD), F32)
    p_copies = []

    def spread(i, total, along):
        hh = (h + i) % HEADS
        part = nt(dproj[...], wi[pl.ds(pl.multiple_of(hh * HD, HD), HD), :])
        if i:
            ps[i] = part.astype(BF16)
            copy = push(ps.at[i], pr.at[i], p_s.at[i], p_r.at[i], at_head(i))
            copy.start()
            p_copies.append((i, copy))
        else:
            own[...] = part
        return total + part, along + part * n8[hh]

    for i in (6, 2, 7, 5, 3, 1, 4, 0):
        total, along = spread(i, total, along)
    lane = lax.broadcasted_iota(jnp.int32, (TOK, HD), 1)
    both = jnp.where(
        lane == 0,
        jnp.sum(total, axis=1, keepdims=True),
        jnp.where(lane == 1, jnp.sum(along, axis=1, keepdims=True), 0.0),
    )
    st[...] = both.T[0:8, :]
    t_copies = [
        push(st, sr.at[i], t_s.at[i], t_r.at[i], at_head(i)) for i in range(1, HEADS)
    ]
    for copy in t_copies:
        copy.start()

    for copy in e_third:
        copy.wait_recv()
    early = add_third(ga2, ge3)
    g1[:, 0:HD] = early[:, 0:HD]
    g2[...] = early[:, HD:]

    l_second.wait_recv()
    add_second(gb1, gl2, gb2)
    l_third = sum_planes(gb2, gl3, (l3_s, l3_r))
    for copy in l_third:
        copy.start()

    summed = own[...]
    for i, copy in p_copies:
        copy.wait_recv()
        summed += pr[i].astype(F32)
    stats = st[...]
    for i in range(1, HEADS):
        t_copies[i - 1].wait_recv()
        stats += sr[i]
    wide = jnp.concatenate([stats, jnp.zeros((HD - 8, TOK), F32)], axis=0).T * (1.0 / WIDTH)
    back = (summed - wide[:, 0:1] - n8[h] * wide[:, 1:2]) * rsd[...]
    gi[...] = (fg[0].astype(F32) + back).astype(BF16)

    for copy in (
        fg_copies + kv_copies + do_copies + dq_copies + e_third + t_copies
    ):
        copy.wait_send()
    for d in range(REACH):
        hop_queries(d).wait_send()
    for i, copy in p_copies:
        copy.wait_send()
    for copy in (e_first, e_second, k_first, k_second, l_first, l_second):
        copy.wait_send()

    for copy in l_third:
        copy.wait_recv()
    late = add_third(gb2, gl3)
    g1[:, HD : 2 * HD] = late[:, 0:HD]
    g1[:, 2 * HD : 3 * HD] = late[:, 2 * HD :]
    g1[:, 3 * HD :] = late[:, HD : 2 * HD]
    for copy in l_third:
        copy.wait_send()


def rows_of(columns):
    return [
        pltpu.VMEM((32, 2, 16, columns), BF16),
        pltpu.VMEM((32, 16, columns), BF16),
        pltpu.VMEM((16, 2, 16, columns), BF16),
        pltpu.VMEM((16, 16, columns), BF16),
        pltpu.VMEM((16, 16, columns), BF16),
        pltpu.VMEM((16, 16, columns), BF16),
    ]


def per_device(events, out_grad, saved_attn, in_weight, out_weight, lengths):
    tile = (TOK, HD)
    vmem = pl.BlockSpec(memory_space=pltpu.VMEM)
    dma = pltpu.SemaphoreType.DMA
    scratch = [
        pltpu.VMEM((TOK, WIDTH), BF16),
        pltpu.VMEM(tile, BF16),
        pltpu.VMEM((WIDTH, 4 * HD), BF16),
        pltpu.VMEM((WIDTH, HD), BF16),
        pltpu.SMEM((NSEQ,), jnp.int32),
        pltpu.VMEM((HEADS,) + tile, F32),
        pltpu.VMEM((TOK, WIDTH), BF16),
        pltpu.VMEM((WIDTH, TOK), BF16),
        pltpu.VMEM(tile, F32),
        pltpu.VMEM((4,) + tile, F32),
        pltpu.VMEM(tile, F32),
        pltpu.VMEM(tile, F32),
        pltpu.VMEM(tile, F32),
        pltpu.VMEM((TOK, 4 * HD), BF16),
        pltpu.VMEM((HEADS,) + tile, BF16),
        pltpu.VMEM((REACH + 1,) + tile, BF16),
        pltpu.VMEM((REACH + 1,) + tile, BF16),
        pltpu.VMEM((4, 2) + tile, BF16),
        pltpu.VMEM((HD, 4 * TOK), BF16),
        pltpu.VMEM((REACH + 1, 8, TOK), jnp.int32),
        pltpu.VMEM((4 * TOK, HD), jnp.int32),
        pltpu.VMEM((4, 2) + tile, F32),
        pltpu.VMEM((REACH + 1, HD, TOK), BF16),
        pltpu.VMEM((REACH + 1, HD, TOK), BF16),
        pltpu.VMEM((2, 2) + tile, BF16),
        pltpu.VMEM((2, 2) + tile, BF16),
        pltpu.VMEM((2,) + tile, BF16),
        pltpu.VMEM((2,) + tile, BF16),
        *rows_of(2 * HD),
        *rows_of(3 * HD),
        pltpu.VMEM((HEADS,) + tile, BF16),
        pltpu.VMEM((HEADS,) + tile, BF16),
        pltpu.VMEM(tile, F32),
        pltpu.VMEM((8, TOK), F32),
        pltpu.VMEM((HEADS, 8, TOK), F32),
    ]
    counts = (8, 8, 5, 5, 5, 5, 4, 4, 5, 5, 2, 2, 2, 2, 16, 16, 2, 2, 16, 16, 8, 8, 8, 8)
    scratch += [dma((6,)), pltpu.SemaphoreType.REGULAR((3,))]
    scratch += [dma((n,)) for n in counts]
    return pl.pallas_call(
        kernel,
        out_shape=(
            jax.ShapeDtypeStruct(tile, BF16),
            jax.ShapeDtypeStruct((16, 4 * HD), F32),
            jax.ShapeDtypeStruct((16, HD), F32),
        ),
        in_specs=[pl.BlockSpec(memory_space=pl.ANY)] * 6,
        out_specs=(vmem,) * 3,
        scratch_shapes=scratch,
        compiler_params=pltpu.CompilerParams(
            collective_id=0, has_side_effects=True, vmem_limit_bytes=56 * 2**20
        ),
        name="layer_backward",
    )(events, out_grad, saved_attn, in_weight, out_weight, lengths)


def solution(mesh):
    return jax.shard_map(
        per_device,
        mesh=mesh,
        in_specs=(
            P("seq", None),
            P("seq", "head"),
            P("seq", "head"),
            P(None, "head"),
            P(None, "head"),
            P(),
        ),
        out_specs=(P("seq", "head"), P("seq", "head"), P("seq", "head")),
        check_vma=False,
    )
```

```python
import math

import jax
import jax.numpy as jnp
from jax import lax
from jax.experimental import pallas as pl
from jax.experimental.pallas import tpu as pltpu
from jax.sharding import PartitionSpec as P

HEADS = 8
HD = 128
TOK = 256
WIDTH = 1024
PLANES = 16
NSEQ = 16
REACH = 4
MOST = 4096.0
EPS = 1e-05
SCALE = 1.0 / math.sqrt(HD)
GRAD_SCALE = 1.0 / 128.0
MESH = pl.DeviceIdType.MESH
F32 = jnp.float32
BF16 = jnp.bfloat16
NEAR_LAST = (8, 7, 9, 6, 10, 5, 11, 4, 12, 3, 13, 2, 14, 1, 15)


def nn(a, b):
    return jnp.dot(a, b, preferred_element_type=F32)


def nt(a, b):
    return lax.dot_general(a, b, (((1,), (1,)), ((), ())), preferred_element_type=F32)


def tn(a, b):
    return lax.dot_general(a, b, (((0,), (0,)), ((), ())), preferred_element_type=F32)


def push(src, dst, sent, came, device):
    return pltpu.make_async_remote_copy(
        src_ref=src,
        dst_ref=dst,
        send_sem=sent,
        recv_sem=came,
        device_id=device,
        device_id_type=MESH,
    )


def kernel(
    ev_h, og_h, sa_h, wi_h, wo_h, lens_h, gi, g1, g2,
    ev, sa, wi, wo, lens,
    n8, nb, ntr, rsd, slope, upart, ahat_s, arstd_s, dproj,
    fg, qa, doa, kva, ktr, begin, rowpos, kvg, dqs, dqr,
    kvs1, kvr1, kvs2, kvr2,
    ge, ge1, ga1, ge2, ga2, ge3,
    gl, gl1, gb1, gl2, gb2, gl3,
    ps, pr, own, st, sr,
    in_s, near,
    fg_s, fg_r, q_s, q_r, do_s, do_r, kv_s, kv_r, dq_s, dq_r, kx_s, kx_r,
    e12_s, e12_r, e3_s, e3_r, l12_s, l12_r, l3_s, l3_r, p_s, p_r, t_s, t_r,
):
    s = lax.axis_index("seq")
    h = lax.axis_index("head")
    z = s // 4
    xh = (s // 2) % 2
    c = s % 2

    def at_z(i):
        return (((z + i) % PLANES) * 4 + xh * 2 + c, h)

    def in_plane(i):
        return (z * 4 + ((xh + i // 2) % 2) * 2 + (c + i % 2) % 2, h)

    def at_head(i):
        return (s, (h + i) % HEADS)

    barrier = pltpu.get_barrier_semaphore()
    for i in range(1, HEADS):
        pl.semaphore_signal(barrier, inc=1, device_id=at_head(i), device_id_type=MESH)
    for i in range(1, 4):
        pl.semaphore_signal(barrier, inc=1, device_id=in_plane(i), device_id_type=MESH)
    for i in (1, PLANES - 1):
        pl.semaphore_signal(barrier, inc=1, device_id=at_z(i), device_id_type=MESH)

    def greet(level, distance):
        for i in (distance, PLANES - distance):
            pl.semaphore_signal(
                near.at[level], inc=1, device_id=at_z(i), device_id_type=MESH
            )

    loads = [
        pltpu.make_async_copy(src, dst, in_s.at[i])
        for i, (src, dst) in enumerate(
            ((og_h, fg.at[0]), (ev_h, ev), (wi_h, wi), (wo_h, wo), (sa_h, sa), (lens_h, lens))
        )
    ]
    for copy in loads:
        copy.start()

    def norm_rows(i, carry):
        r = pl.multiple_of(i * 64, 64)
        x = ev[pl.ds(r, 64), :].astype(F32)
        cent = x - jnp.mean(x, axis=1, keepdims=True)
        rstd = lax.rsqrt(jnp.mean(cent * cent, axis=1, keepdims=True) + EPS)
        normed = cent * rstd
        nb[pl.ds(r, 64), :] = normed.astype(BF16)
        for j in range(HEADS):
            n8[j, pl.ds(r, 64), :] = normed[:, j * HD : (j + 1) * HD]
        rsd[pl.ds(r, 64), :] = jnp.broadcast_to(rstd, (64, HD))
        return carry

    loads[1].wait()
    lax.fori_loop(0, 2, norm_rows, 0)

    loads[0].wait()
    pl.semaphore_wait(barrier, HEADS - 1 + 3 + 2)
    greet(0, 1)
    fg_copies = [
        push(fg.at[0], fg.at[i], fg_s.at[i], fg_r.at[i], at_head(i)) for i in range(1, HEADS)
    ]
    for i in (6, 2, 7, 5, 3, 1, 4):
        fg_copies[i - 1].start()

    lax.fori_loop(2, 4, norm_rows, 0)
    pl.semaphore_wait(near.at[0], 2)
    greet(1, 2)

    def hop_queries(d, by):
        return push(
            qa.at[d], qa.at[d + by], q_s.at[d + by], q_r.at[d + by], at_z(PLANES - by)
        )

    loads[2].wait()
    for part in (3, 1, 2, 0):
        proj = nn(nb[...], wi[:, part * HD : (part + 1) * HD])
        sig = 0.5 * jnp.tanh(0.5 * proj) + 0.5
        act = (proj * sig).astype(BF16)
        slope[part] = sig * (1.0 + proj * (1.0 - sig))
        if part == 0:
            upart[...] = act.astype(F32)
        elif part == 1:
            kva[0, 1] = act
        elif part == 2:
            qa[0] = act
        else:
            kva[0, 0] = act
        if part == 1:
            kv_copies = [
                push(kva.at[0], kva.at[i], kv_s.at[i], kv_r.at[i], in_plane(i))
                for i in (3, 2, 1)
            ]
            for copy in kv_copies:
                copy.start()
        elif part == 2:
            hop_queries(0, 2).start()
            hop_queries(0, 1).start()

    loads[4].wait()
    attn = sa[...].astype(F32)
    cent = attn - jnp.mean(attn, axis=1, keepdims=True)
    arstd = lax.rsqrt(jnp.mean(cent * cent, axis=1, keepdims=True) + EPS)
    ahat_s[...] = cent * arstd
    arstd_s[...] = jnp.broadcast_to(arstd, (TOK, HD))
    pl.semaphore_wait(near.at[1], 2)
    greet(2, 4)

    loads[3].wait()
    dout = nn(fg[0], wo[pl.ds(pl.multiple_of(h * HD, HD), HD), :])
    for i in (1, 7, 4, 2, 6, 3, 5):
        fg_copies[i - 1].wait_recv()
        row = pl.multiple_of(((h + HEADS - i) % HEADS) * HD, HD)
        dout += nn(fg[i], wo[pl.ds(row, HD), :])
    ahat = ahat_s[...]
    dnorm = dout * upart[...]
    doa[0] = (
        (
            dnorm
            - jnp.mean(dnorm, axis=1, keepdims=True)
            - ahat * jnp.mean(dnorm * ahat, axis=1, keepdims=True)
        )
        * arstd_s[...]
    ).astype(BF16)
    def hop_upstream(d, by):
        return push(
            doa.at[d], doa.at[d + by], do_s.at[d + by], do_r.at[d + by], at_z(PLANES - by)
        )

    hop_upstream(0, 2).start()
    hop_upstream(0, 1).start()
    hop_queries(0, 2).wait_recv()
    hop_queries(2, 2).start()
    hop_queries(0, 1).wait_recv()
    hop_queries(1, 2).start()

    def turn_columns(j, carry):
        ntr[pl.ds(pl.multiple_of(j * HD, HD), HD), :] = n8[j].T.astype(BF16)
        return carry

    lax.fori_loop(0, HEADS, turn_columns, 0)

    dproj[:, 0:HD] = (dout * ahat * slope[0]).astype(BF16)
    gated = (ahat * upart[...]).astype(BF16)
    ge[:, :, :, 0:HD] = (nn(ntr[...], dproj[:, 0:HD])).astype(BF16).reshape(32, 2, 16, HD)

    def head_rows(i, carry):
        block = pl.ds(((h + HEADS - i) % HEADS) * 4, 4)
        ge[block, :, :, HD : 2 * HD] = tn(fg[i], gated).astype(BF16).reshape(4, 2, 16, HD)
        return carry

    lax.fori_loop(0, HEADS, head_rows, 0)

    def sum_parts(whole, into, over):
        return push(whole.at[:, 1 - c], into, over[0].at[0], over[1].at[0], in_plane(1))

    def add_first(whole, came, kept):
        def step(i, carry):
            kept[i] = (
                whole[pl.ds(2 * i, 2), c].astype(F32) + came[pl.ds(2 * i, 2)].astype(F32)
            ).astype(BF16)
            return carry

        lax.fori_loop(0, PLANES, step, 0)

    def sum_across(kept, into, over):
        return push(kept.at[:, 1 - xh], into, over[0].at[1], over[1].at[1], in_plane(2))

    def add_second(kept, came, final):
        def step(i, carry):
            final[i] = (kept[i, xh].astype(F32) + came[i].astype(F32)).astype(BF16)
            return carry

        lax.fori_loop(0, PLANES, step, 0)

    def sum_planes(final, into, over):
        return [
            push(final.at[(z + i) % PLANES], into.at[i], over[0].at[i], over[1].at[i], at_z(i))
            for i in NEAR_LAST
        ]

    def add_third(final, came):
        total = final[z].astype(F32)
        for i in range(1, PLANES):
            total += came[i].astype(F32)
        return total * GRAD_SCALE

    e_first = sum_parts(ge, ge1, (e12_s, e12_r))
    e_first.start()

    loads[5].wait()
    ends = []
    run = 0
    for i in range(NSEQ):
        run = run + lens[i]
        ends.append(run)
    own_plane = (z + PLANES // 2) % PLANES

    def history_starts(d, carry):
        plane = own_plane + d
        qpos = plane * 1024 + xh * 512 + c * 256 + lax.broadcasted_iota(jnp.int32, (8, TOK), 1)
        first = jnp.zeros((8, TOK), jnp.int32)
        for end in ends:
            first = jnp.maximum(first, jnp.where(qpos >= end, end, 0))
        begin[d] = jnp.where(plane < PLANES, first - own_plane * 1024, 2 * 1024)
        return carry

    lax.fori_loop(0, REACH + 1, history_starts, 0)

    for copy in kv_copies:
        copy.wait_recv()
    for i in range(4):
        ktr[:, i * TOK : (i + 1) * TOK] = kva[i, 0].astype(F32).T.astype(BF16)

    def slot_rows(shape):
        row = lax.broadcasted_iota(jnp.int32, shape, 0)
        half = row // 512
        quarter = (row // 256) % 2
        place = jnp.where(xh == 0, half, 1 - half) * 512
        place += jnp.where(c == 0, quarter, 1 - quarter) * 256
        return place + row % 256

    rowpos[...] = slot_rows((4 * TOK, HD))

    def attend(d, same):
        queries = qa[d]
        upstream = doa[d]
        keys = kva[:, 0].reshape(4 * TOK, HD)
        values = kva[:, 1].reshape(4 * TOK, HD)
        down = jnp.concatenate([rowpos[...]] * 2, axis=1)
        mask = down >= begin[d, 0:1, :]
        if same:
            lane = lax.broadcasted_iota(jnp.int32, (1, TOK), 1)
            mask = mask & (down <= xh * 512 + c * 256 + lane)
        half = nt(keys, queries) * (0.5 * SCALE)
        bell = 1.0 + jnp.tanh(half)
        weight = half * bell
        sig = 0.5 * bell
        dprob = nt(values, upstream)
        dscore = jnp.where(mask, dprob * (sig + weight * (1.0 - sig)), 0.0).astype(BF16)
        weight = jnp.where(mask, weight, 0.0).astype(BF16)
        grad_k = nn(dscore, queries).reshape(4, TOK, HD)
        grad_v = nn(weight, upstream).reshape(4, TOK, HD)
        if same:
            kvg[:, 0] = grad_k
            kvg[:, 1] = grad_v
        else:
            kvg[:, 0] += grad_k
            kvg[:, 1] += grad_v
        dqs[d] = nn(ktr[...], dscore).astype(BF16)

    hop_upstream(0, 2).wait_recv()
    hop_upstream(2, 2).start()
    hop_upstream(0, 1).wait_recv()
    hop_upstream(1, 2).start()
    attend(0, True)

    e_first.wait_recv()
    add_first(ge, ge1, ga1)
    e_second = sum_across(ga1, ge2, (e12_s, e12_r))
    e_second.start()

    def attend_step(turn, carry):
        d = jnp.where(turn < 2, 2 - turn, 6 - turn)

        @pl.when(d == 4)
        def _():
            hop_queries(2, 2).wait_recv()
            hop_upstream(2, 2).wait_recv()

        @pl.when(d == 3)
        def _():
            hop_queries(1, 2).wait_recv()
            hop_upstream(1, 2).wait_recv()

        attend(d, False)
        push(dqs.at[d], dqr.at[d], dq_s.at[d], dq_r.at[d], at_z(d)).start()
        return carry

    lax.fori_loop(0, REACH, attend_step, 0)

    for j in range(2):
        other = 2 * j + 1
        kvs1[j] = kvg[other].astype(BF16)
    k_first = push(kvs1, kvr1, kx_s.at[0], kx_r.at[0], in_plane(1))
    k_first.start()


    k_first.wait_recv()
    kvs2[...] = (kvg[2] + kvr1[1].astype(F32)).astype(BF16)
    k_second = push(kvs2, kvr2, kx_s.at[1], kx_r.at[1], in_plane(2))
    k_second.start()

    dq_copies = [
        push(dqs.at[d], dqr.at[d], dq_s.at[d], dq_r.at[d], at_z(d)) for d in range(1, REACH + 1)
    ]
    grad_q = dqs[0].astype(F32)
    for d in range(REACH, 0, -1):
        dq_copies[d - 1].wait_recv()
        grad_q += dqr[d].astype(F32)
    dproj[:, 2 * HD : 3 * HD] = (grad_q.T * (SCALE / MOST) * slope[2]).astype(BF16)
    gl[:, :, :, 2 * HD :] = (
        nn(ntr[...], dproj[:, 2 * HD : 3 * HD]).astype(BF16).reshape(32, 2, 16, HD)
    )

    k_second.wait_recv()
    grad_k = kvg[0, 0] + kvr1[0, 0].astype(F32) + kvr2[0].astype(F32)
    grad_v = kvg[0, 1] + kvr1[0, 1].astype(F32) + kvr2[1].astype(F32)
    dproj[:, 3 * HD :] = (grad_k * (SCALE / MOST) * slope[3]).astype(BF16)
    dproj[:, HD : 2 * HD] = (grad_v * (1.0 / MOST) * slope[1]).astype(BF16)
    pair = jnp.concatenate([dproj[:, HD : 2 * HD], dproj[:, 3 * HD :]], axis=1)
    gl[:, :, :, 0 : 2 * HD] = nn(ntr[...], pair).astype(BF16).reshape(32, 2, 16, 2 * HD)
    l_first = sum_parts(gl, gl1, (l12_s, l12_r))
    l_first.start()
    l_first.wait_recv()
    add_first(gl, gl1, gb1)
    l_second = sum_across(gb1, gl2, (l12_s, l12_r))
    l_second.start()
    e_second.wait_recv()
    add_second(ga1, ge2, ga2)
    pl.semaphore_wait(near.at[2], 2)
    e_third = sum_planes(ga2, ge3, (e3_s, e3_r))
    for copy in e_third:
        copy.start()

    total = jnp.zeros((TOK, HD), F32)
    along = jnp.zeros((TOK, HD), F32)
    p_copies = []

    def spread(i, total, along):
        hh = (h + i) % HEADS
        part = nt(dproj[...], wi[pl.ds(pl.multiple_of(hh * HD, HD), HD), :])
        if i:
            ps[i] = part.astype(BF16)
            copy = push(ps.at[i], pr.at[i], p_s.at[i], p_r.at[i], at_head(i))
            copy.start()
            p_copies.append((i, copy))
        else:
            own[...] = part
        return total + part, along + part * n8[hh]

    for i in (6, 2, 7, 5, 3, 1, 4, 0):
        total, along = spread(i, total, along)
    lane = lax.broadcasted_iota(jnp.int32, (TOK, HD), 1)
    both = jnp.where(
        lane == 0,
        jnp.sum(total, axis=1, keepdims=True),
        jnp.where(lane == 1, jnp.sum(along, axis=1, keepdims=True), 0.0),
    )
    st[...] = both.T[0:8, :]
    t_copies = [
        push(st, sr.at[i], t_s.at[i], t_r.at[i], at_head(i)) for i in range(1, HEADS)
    ]
    for copy in t_copies:
        copy.start()

    for copy in e_third:
        copy.wait_recv()
    early = add_third(ga2, ge3)
    g1[:, 0:HD] = early[:, 0:HD]
    g2[...] = early[:, HD:]

    l_second.wait_recv()
    add_second(gb1, gl2, gb2)
    l_third = sum_planes(gb2, gl3, (l3_s, l3_r))
    for copy in l_third:
        copy.start()

    summed = own[...]
    for i, copy in p_copies:
        copy.wait_recv()
        summed += pr[i].astype(F32)
    stats = st[...]
    for i in range(1, HEADS):
        t_copies[i - 1].wait_recv()
        stats += sr[i]
    wide = jnp.concatenate([stats, jnp.zeros((HD - 8, TOK), F32)], axis=0).T * (1.0 / WIDTH)
    back = (summed - wide[:, 0:1] - n8[h] * wide[:, 1:2]) * rsd[...]
    gi[...] = (fg[0].astype(F32) + back).astype(BF16)

    for copy in (
        fg_copies + kv_copies + dq_copies + e_third + t_copies
    ):
        copy.wait_send()
    for d, by in ((0, 1), (0, 2), (1, 2), (2, 2)):
        hop_queries(d, by).wait_send()
        hop_upstream(d, by).wait_send()
    for i, copy in p_copies:
        copy.wait_send()
    for copy in (e_first, e_second, k_first, k_second, l_first, l_second):
        copy.wait_send()

    for copy in l_third:
        copy.wait_recv()
    late = add_third(gb2, gl3)
    g1[:, HD : 2 * HD] = late[:, 0:HD]
    g1[:, 2 * HD : 3 * HD] = late[:, 2 * HD :]
    g1[:, 3 * HD :] = late[:, HD : 2 * HD]
    for copy in l_third:
        copy.wait_send()


def rows_of(columns):
    return [
        pltpu.VMEM((32, 2, 16, columns), BF16),
        pltpu.VMEM((32, 16, columns), BF16),
        pltpu.VMEM((16, 2, 16, columns), BF16),
        pltpu.VMEM((16, 16, columns), BF16),
        pltpu.VMEM((16, 16, columns), BF16),
        pltpu.VMEM((16, 16, columns), BF16),
    ]


def per_device(events, out_grad, saved_attn, in_weight, out_weight, lengths):
    tile = (TOK, HD)
    vmem = pl.BlockSpec(memory_space=pltpu.VMEM)
    dma = pltpu.SemaphoreType.DMA
    scratch = [
        pltpu.VMEM((TOK, WIDTH), BF16),
        pltpu.VMEM(tile, BF16),
        pltpu.VMEM((WIDTH, 4 * HD), BF16),
        pltpu.VMEM((WIDTH, HD), BF16),
        pltpu.SMEM((NSEQ,), jnp.int32),
        pltpu.VMEM((HEADS,) + tile, F32),
        pltpu.VMEM((TOK, WIDTH), BF16),
        pltpu.VMEM((WIDTH, TOK), BF16),
        pltpu.VMEM(tile, F32),
        pltpu.VMEM((4,) + tile, F32),
        pltpu.VMEM(tile, F32),
        pltpu.VMEM(tile, F32),
        pltpu.VMEM(tile, F32),
        pltpu.VMEM((TOK, 4 * HD), BF16),
        pltpu.VMEM((HEADS,) + tile, BF16),
        pltpu.VMEM((REACH + 1,) + tile, BF16),
        pltpu.VMEM((REACH + 1,) + tile, BF16),
        pltpu.VMEM((4, 2) + tile, BF16),
        pltpu.VMEM((HD, 4 * TOK), BF16),
        pltpu.VMEM((REACH + 1, 8, TOK), jnp.int32),
        pltpu.VMEM((4 * TOK, HD), jnp.int32),
        pltpu.VMEM((4, 2) + tile, F32),
        pltpu.VMEM((REACH + 1, HD, TOK), BF16),
        pltpu.VMEM((REACH + 1, HD, TOK), BF16),
        pltpu.VMEM((2, 2) + tile, BF16),
        pltpu.VMEM((2, 2) + tile, BF16),
        pltpu.VMEM((2,) + tile, BF16),
        pltpu.VMEM((2,) + tile, BF16),
        *rows_of(2 * HD),
        *rows_of(3 * HD),
        pltpu.VMEM((HEADS,) + tile, BF16),
        pltpu.VMEM((HEADS,) + tile, BF16),
        pltpu.VMEM(tile, F32),
        pltpu.VMEM((8, TOK), F32),
        pltpu.VMEM((HEADS, 8, TOK), F32),
    ]
    counts = (8, 8, 5, 5, 5, 5, 4, 4, 5, 5, 2, 2, 2, 2, 16, 16, 2, 2, 16, 16, 8, 8, 8, 8)
    scratch += [dma((6,)), pltpu.SemaphoreType.REGULAR((3,))]
    scratch += [dma((n,)) for n in counts]
    return pl.pallas_call(
        kernel,
        out_shape=(
            jax.ShapeDtypeStruct(tile, BF16),
            jax.ShapeDtypeStruct((16, 4 * HD), F32),
            jax.ShapeDtypeStruct((16, HD), F32),
        ),
        in_specs=[pl.BlockSpec(memory_space=pl.ANY)] * 6,
        out_specs=(vmem,) * 3,
        scratch_shapes=scratch,
        compiler_params=pltpu.CompilerParams(
            collective_id=0, has_side_effects=True, vmem_limit_bytes=56 * 2**20
        ),
        name="layer_backward",
    )(events, out_grad, saved_attn, in_weight, out_weight, lengths)


def solution(mesh):
    return jax.shard_map(
        per_device,
        mesh=mesh,
        in_specs=(
            P("seq", None),
            P("seq", "head"),
            P("seq", "head"),
            P(None, "head"),
            P(None, "head"),
            P(),
        ),
        out_specs=(P("seq", "head"), P("seq", "head"), P("seq", "head")),
        check_vma=False,
    )
```

```python
import math

import jax
import jax.numpy as jnp
from jax import lax
from jax.experimental import pallas as pl
from jax.experimental.pallas import tpu as pltpu
from jax.sharding import PartitionSpec as P

HEADS = 8
HD = 128
TOK = 256
WIDTH = 1024
PLANES = 16
NSEQ = 16
REACH = 4
MOST = 4096.0
EPS = 1e-05
SCALE = 1.0 / math.sqrt(HD)
GRAD_SCALE = 1.0 / 128.0
MESH = pl.DeviceIdType.MESH
F32 = jnp.float32
BF16 = jnp.bfloat16
NEAR_LAST = (8, 7, 9, 6, 10, 5, 11, 4, 12, 3, 13, 2, 14, 1, 15)
FAR = 4
FAR_COUNT = 9


def nn(a, b):
    return jnp.dot(a, b, preferred_element_type=F32)


def nt(a, b):
    return lax.dot_general(a, b, (((1,), (1,)), ((), ())), preferred_element_type=F32)


def tn(a, b):
    return lax.dot_general(a, b, (((0,), (0,)), ((), ())), preferred_element_type=F32)


def push(src, dst, sent, came, device):
    return pltpu.make_async_remote_copy(
        src_ref=src,
        dst_ref=dst,
        send_sem=sent,
        recv_sem=came,
        device_id=device,
        device_id_type=MESH,
    )


def kernel(
    ev_h, og_h, sa_h, wi_h, wo_h, lens_h, gi, g1, g2,
    ev, sa, wi, wo, lens,
    n8, nb, ntr, rsd, slope, upart, ahat_s, arstd_s, dproj,
    fg, qa, doa, kva, ktr, begin, rowpos, kvg, dqs, dqr,
    kvs1, kvr1, kvs2, kvr2,
    ge, ge1, ga1, ge2, ga2, ge3,
    gl, gl1, gb1, gl2, gb2, gl3,
    ps, pr, own, st, sr,
    in_s, near,
    fg_s, fg_r, q_s, q_r, do_s, do_r, kv_s, kv_r, dq_s, dq_r, kx_s, kx_r,
    e12_s, e12_r, e3_s, e3_r, l12_s, l12_r, l3_s, l3_r, p_s, p_r, t_s, t_r,
):
    s = lax.axis_index("seq")
    h = lax.axis_index("head")
    z = s // 4
    xh = (s // 2) % 2
    c = s % 2

    def at_z(i):
        return (((z + i) % PLANES) * 4 + xh * 2 + c, h)

    def in_plane(i):
        return (z * 4 + ((xh + i // 2) % 2) * 2 + (c + i % 2) % 2, h)

    def at_head(i):
        return (s, (h + i) % HEADS)

    barrier = pltpu.get_barrier_semaphore()
    for i in range(1, HEADS):
        pl.semaphore_signal(barrier, inc=1, device_id=at_head(i), device_id_type=MESH)
    for i in range(1, 4):
        pl.semaphore_signal(barrier, inc=1, device_id=in_plane(i), device_id_type=MESH)
    for i in (1, PLANES - 1):
        pl.semaphore_signal(barrier, inc=1, device_id=at_z(i), device_id_type=MESH)

    def greet(level, distance):
        for i in (distance, PLANES - distance):
            pl.semaphore_signal(
                near.at[level], inc=1, device_id=at_z(i), device_id_type=MESH
            )

    loads = [
        pltpu.make_async_copy(src, dst, in_s.at[i])
        for i, (src, dst) in enumerate(
            ((og_h, fg.at[0]), (ev_h, ev), (wi_h, wi), (wo_h, wo), (sa_h, sa), (lens_h, lens))
        )
    ]
    for copy in loads:
        copy.start()

    def norm_rows(i, carry):
        r = pl.multiple_of(i * 64, 64)
        x = ev[pl.ds(r, 64), :].astype(F32)
        cent = x - jnp.mean(x, axis=1, keepdims=True)
        rstd = lax.rsqrt(jnp.mean(cent * cent, axis=1, keepdims=True) + EPS)
        normed = cent * rstd
        nb[pl.ds(r, 64), :] = normed.astype(BF16)
        for j in range(HEADS):
            n8[j, pl.ds(r, 64), :] = normed[:, j * HD : (j + 1) * HD]
        rsd[pl.ds(r, 64), :] = jnp.broadcast_to(rstd, (64, HD))
        return carry

    loads[1].wait()
    lax.fori_loop(0, 2, norm_rows, 0)

    loads[0].wait()
    pl.semaphore_wait(barrier, HEADS - 1 + 3 + 2)
    greet(0, 1)
    fg_copies = [
        push(fg.at[0], fg.at[i], fg_s.at[i], fg_r.at[i], at_head(i)) for i in range(1, HEADS)
    ]
    for i in (6, 2, 7, 5, 3, 1, 4):
        fg_copies[i - 1].start()

    lax.fori_loop(2, 4, norm_rows, 0)
    pl.semaphore_wait(near.at[0], 2)
    greet(1, 2)

    def hop_queries(d, by):
        return push(
            qa.at[d], qa.at[d + by], q_s.at[d + by], q_r.at[d + by], at_z(PLANES - by)
        )

    loads[2].wait()
    for part in (3, 1, 2, 0):
        proj = nn(nb[...], wi[:, part * HD : (part + 1) * HD])
        sig = 0.5 * jnp.tanh(0.5 * proj) + 0.5
        act = (proj * sig).astype(BF16)
        slope[part] = sig * (1.0 + proj * (1.0 - sig))
        if part == 0:
            upart[...] = act.astype(F32)
        elif part == 1:
            kva[0, 1] = act
        elif part == 2:
            qa[0] = act
        else:
            kva[0, 0] = act
        if part == 1:
            kv_copies = [
                push(kva.at[0], kva.at[i], kv_s.at[i], kv_r.at[i], in_plane(i))
                for i in (3, 2, 1)
            ]
            for copy in kv_copies:
                copy.start()
        elif part == 2:
            hop_queries(0, 2).start()
            hop_queries(0, 1).start()

    loads[4].wait()
    attn = sa[...].astype(F32)
    cent = attn - jnp.mean(attn, axis=1, keepdims=True)
    arstd = lax.rsqrt(jnp.mean(cent * cent, axis=1, keepdims=True) + EPS)
    ahat_s[...] = cent * arstd
    arstd_s[...] = jnp.broadcast_to(arstd, (TOK, HD))
    pl.semaphore_wait(near.at[1], 2)
    greet(2, 4)

    loads[3].wait()
    dout = nn(fg[0], wo[pl.ds(pl.multiple_of(h * HD, HD), HD), :])
    for i in (1, 7, 4, 2, 6, 3, 5):
        fg_copies[i - 1].wait_recv()
        row = pl.multiple_of(((h + HEADS - i) % HEADS) * HD, HD)
        dout += nn(fg[i], wo[pl.ds(row, HD), :])
    ahat = ahat_s[...]
    dnorm = dout * upart[...]
    doa[0] = (
        (
            dnorm
            - jnp.mean(dnorm, axis=1, keepdims=True)
            - ahat * jnp.mean(dnorm * ahat, axis=1, keepdims=True)
        )
        * arstd_s[...]
    ).astype(BF16)
    def hop_upstream(d, by):
        return push(
            doa.at[d], doa.at[d + by], do_s.at[d + by], do_r.at[d + by], at_z(PLANES - by)
        )

    hop_upstream(0, 2).start()
    hop_upstream(0, 1).start()
    hop_queries(0, 2).wait_recv()
    hop_queries(2, 2).start()
    hop_queries(0, 1).wait_recv()
    hop_queries(1, 2).start()

    def turn_columns(j, carry):
        ntr[pl.ds(pl.multiple_of(j * HD, HD), HD), :] = n8[j].T.astype(BF16)
        return carry

    lax.fori_loop(0, HEADS, turn_columns, 0)

    dproj[:, 0:HD] = (dout * ahat * slope[0]).astype(BF16)
    gated = (ahat * upart[...]).astype(BF16)
    ge[:, :, :, 0:HD] = (nn(ntr[...], dproj[:, 0:HD])).astype(BF16).reshape(32, 2, 16, HD)

    def head_rows(i, carry):
        block = pl.ds(((h + HEADS - i) % HEADS) * 4, 4)
        ge[block, :, :, HD : 2 * HD] = tn(fg[i], gated).astype(BF16).reshape(4, 2, 16, HD)
        return carry

    lax.fori_loop(0, HEADS, head_rows, 0)

    def sum_parts(whole, into, over):
        return push(whole.at[:, 1 - c], into, over[0].at[0], over[1].at[0], in_plane(1))

    def add_first(whole, came, kept):
        def step(k, carry):
            rows = pl.ds(2 * ((z + k + FAR) % PLANES), 2)
            kept[k] = (whole[rows, c].astype(F32) + came[rows].astype(F32)).astype(BF16)
            return carry

        lax.fori_loop(0, PLANES, step, 0)

    def sum_across(kept, into, over):
        return [
            push(
                kept.at[pl.ds(low, count), 1 - xh],
                into.at[pl.ds(low, count)],
                over[0].at[i],
                over[1].at[i],
                in_plane(2),
            )
            for i, low, count in ((1, 0, FAR_COUNT), (2, FAR_COUNT, PLANES - FAR_COUNT))
        ]

    def add_second(kept, came, final, low, high):
        def step(k, carry):
            final[k] = (kept[k, xh].astype(F32) + came[k].astype(F32)).astype(BF16)
            return carry

        lax.fori_loop(low, high, step, 0)

    def sum_planes(final, into, over):
        return [
            push(
                final.at[(i - FAR) % PLANES], into.at[i], over[0].at[i], over[1].at[i], at_z(i)
            )
            for i in NEAR_LAST
        ]

    def add_third(final, came):
        total = final[PLANES - FAR].astype(F32)
        for i in range(1, PLANES):
            total += came[i].astype(F32)
        return total * GRAD_SCALE

    e_first = sum_parts(ge, ge1, (e12_s, e12_r))
    e_first.start()

    loads[5].wait()
    ends = []
    run = 0
    for i in range(NSEQ):
        run = run + lens[i]
        ends.append(run)
    own_plane = (z + PLANES // 2) % PLANES

    def history_starts(d, carry):
        plane = own_plane + d
        qpos = plane * 1024 + xh * 512 + c * 256 + lax.broadcasted_iota(jnp.int32, (8, TOK), 1)
        first = jnp.zeros((8, TOK), jnp.int32)
        for end in ends:
            first = jnp.maximum(first, jnp.where(qpos >= end, end, 0))
        begin[d] = jnp.where(plane < PLANES, first - own_plane * 1024, 2 * 1024)
        return carry

    lax.fori_loop(0, REACH + 1, history_starts, 0)

    for copy in kv_copies:
        copy.wait_recv()
    for i in range(4):
        ktr[:, i * TOK : (i + 1) * TOK] = kva[i, 0].astype(F32).T.astype(BF16)

    def slot_rows(shape):
        row = lax.broadcasted_iota(jnp.int32, shape, 0)
        half = row // 512
        quarter = (row // 256) % 2
        place = jnp.where(xh == 0, half, 1 - half) * 512
        place += jnp.where(c == 0, quarter, 1 - quarter) * 256
        return place + row % 256

    rowpos[...] = slot_rows((4 * TOK, HD))

    def attend(d, same):
        queries = qa[d]
        upstream = doa[d]
        keys = kva[:, 0].reshape(4 * TOK, HD)
        values = kva[:, 1].reshape(4 * TOK, HD)
        down = jnp.concatenate([rowpos[...]] * 2, axis=1)
        mask = down >= begin[d, 0:1, :]
        if same:
            lane = lax.broadcasted_iota(jnp.int32, (1, TOK), 1)
            mask = mask & (down <= xh * 512 + c * 256 + lane)
        half = nt(keys, queries) * (0.5 * SCALE)
        bell = 1.0 + jnp.tanh(half)
        weight = half * bell
        sig = 0.5 * bell
        dprob = nt(values, upstream)
        dscore = jnp.where(mask, dprob * (sig + weight * (1.0 - sig)), 0.0).astype(BF16)
        weight = jnp.where(mask, weight, 0.0).astype(BF16)
        grad_k = nn(dscore, queries).reshape(4, TOK, HD)
        grad_v = nn(weight, upstream).reshape(4, TOK, HD)
        if same:
            kvg[:, 0] = grad_k
            kvg[:, 1] = grad_v
        else:
            kvg[:, 0] += grad_k
            kvg[:, 1] += grad_v
        dqs[d] = nn(ktr[...], dscore).astype(BF16)

    hop_upstream(0, 2).wait_recv()
    hop_upstream(2, 2).start()
    hop_upstream(0, 1).wait_recv()
    hop_upstream(1, 2).start()
    attend(0, True)

    e_first.wait_recv()
    add_first(ge, ge1, ga1)
    e_second = sum_across(ga1, ge2, (e12_s, e12_r))
    for copy in e_second:
        copy.start()

    def attend_step(turn, carry):
        d = jnp.where(turn < 2, 2 - turn, 6 - turn)

        @pl.when(d == 4)
        def _():
            hop_queries(2, 2).wait_recv()
            hop_upstream(2, 2).wait_recv()

        @pl.when(d == 3)
        def _():
            hop_queries(1, 2).wait_recv()
            hop_upstream(1, 2).wait_recv()

        attend(d, False)
        push(dqs.at[d], dqr.at[d], dq_s.at[d], dq_r.at[d], at_z(d)).start()
        return carry

    lax.fori_loop(0, REACH, attend_step, 0)

    for j in range(2):
        other = 2 * j + 1
        kvs1[j] = kvg[other].astype(BF16)
    k_first = push(kvs1, kvr1, kx_s.at[0], kx_r.at[0], in_plane(1))
    k_first.start()


    k_first.wait_recv()
    kvs2[...] = (kvg[2] + kvr1[1].astype(F32)).astype(BF16)
    k_second = push(kvs2, kvr2, kx_s.at[1], kx_r.at[1], in_plane(2))
    k_second.start()

    for copy in e_second:
        copy.wait_recv()
    add_second(ga1, ge2, ga2, 0, PLANES)
    pl.semaphore_wait(near.at[2], 2)
    e_third = sum_planes(ga2, ge3, (e3_s, e3_r))
    dq_copies = [
        push(dqs.at[d], dqr.at[d], dq_s.at[d], dq_r.at[d], at_z(d)) for d in range(1, REACH + 1)
    ]
    grad_q = dqs[0].astype(F32)
    for d in range(REACH, 0, -1):
        dq_copies[d - 1].wait_recv()
        grad_q += dqr[d].astype(F32)
    for copy in e_third:
        copy.start()
    dproj[:, 2 * HD : 3 * HD] = (grad_q.T * (SCALE / MOST) * slope[2]).astype(BF16)
    gl[:, :, :, 2 * HD :] = (
        nn(ntr[...], dproj[:, 2 * HD : 3 * HD]).astype(BF16).reshape(32, 2, 16, HD)
    )

    k_second.wait_recv()
    grad_k = kvg[0, 0] + kvr1[0, 0].astype(F32) + kvr2[0].astype(F32)
    grad_v = kvg[0, 1] + kvr1[0, 1].astype(F32) + kvr2[1].astype(F32)
    dproj[:, 3 * HD :] = (grad_k * (SCALE / MOST) * slope[3]).astype(BF16)
    dproj[:, HD : 2 * HD] = (grad_v * (1.0 / MOST) * slope[1]).astype(BF16)
    pair = jnp.concatenate([dproj[:, HD : 2 * HD], dproj[:, 3 * HD :]], axis=1)
    gl[:, :, :, 0 : 2 * HD] = nn(ntr[...], pair).astype(BF16).reshape(32, 2, 16, 2 * HD)
    l_first = sum_parts(gl, gl1, (l12_s, l12_r))
    l_first.start()
    l_first.wait_recv()
    add_first(gl, gl1, gb1)
    l_second = sum_across(gb1, gl2, (l12_s, l12_r))
    for copy in l_second:
        copy.start()

    total = jnp.zeros((TOK, HD), F32)
    along = jnp.zeros((TOK, HD), F32)
    p_copies = []

    def spread(i, total, along):
        hh = (h + i) % HEADS
        part = nt(dproj[...], wi[pl.ds(pl.multiple_of(hh * HD, HD), HD), :])
        if i:
            ps[i] = part.astype(BF16)
            copy = push(ps.at[i], pr.at[i], p_s.at[i], p_r.at[i], at_head(i))
            copy.start()
            p_copies.append((i, copy))
        else:
            own[...] = part
        return total + part, along + part * n8[hh]

    for i in (6, 2, 7, 5, 3, 1, 4, 0):
        total, along = spread(i, total, along)
    lane = lax.broadcasted_iota(jnp.int32, (TOK, HD), 1)
    both = jnp.where(
        lane == 0,
        jnp.sum(total, axis=1, keepdims=True),
        jnp.where(lane == 1, jnp.sum(along, axis=1, keepdims=True), 0.0),
    )
    st[...] = both.T[0:8, :]
    t_copies = [
        push(st, sr.at[i], t_s.at[i], t_r.at[i], at_head(i)) for i in range(1, HEADS)
    ]
    for copy in t_copies:
        copy.start()

    l_third = sum_planes(gb2, gl3, (l3_s, l3_r))
    l_second[0].wait_recv()
    add_second(gb1, gl2, gb2, 0, FAR_COUNT)
    for copy in l_third[:FAR_COUNT]:
        copy.start()
    l_second[1].wait_recv()
    add_second(gb1, gl2, gb2, FAR_COUNT, PLANES)
    for copy in l_third[FAR_COUNT:]:
        copy.start()

    for copy in e_third:
        copy.wait_recv()
    early = add_third(ga2, ge3)
    g1[:, 0:HD] = early[:, 0:HD]
    g2[...] = early[:, HD:]

    summed = own[...]
    for i, copy in p_copies:
        copy.wait_recv()
        summed += pr[i].astype(F32)
    stats = st[...]
    for i in range(1, HEADS):
        t_copies[i - 1].wait_recv()
        stats += sr[i]
    wide = jnp.concatenate([stats, jnp.zeros((HD - 8, TOK), F32)], axis=0).T * (1.0 / WIDTH)
    back = (summed - wide[:, 0:1] - n8[h] * wide[:, 1:2]) * rsd[...]
    gi[...] = (fg[0].astype(F32) + back).astype(BF16)

    for copy in (
        fg_copies + kv_copies + dq_copies + e_third + t_copies
    ):
        copy.wait_send()
    for d, by in ((0, 1), (0, 2), (1, 2), (2, 2)):
        hop_queries(d, by).wait_send()
        hop_upstream(d, by).wait_send()
    for i, copy in p_copies:
        copy.wait_send()
    for copy in e_second + l_second + [e_first, k_first, k_second, l_first]:
        copy.wait_send()

    for copy in l_third:
        copy.wait_recv()
    late = add_third(gb2, gl3)
    g1[:, HD : 2 * HD] = late[:, 0:HD]
    g1[:, 2 * HD : 3 * HD] = late[:, 2 * HD :]
    g1[:, 3 * HD :] = late[:, HD : 2 * HD]
    for copy in l_third:
        copy.wait_send()


def rows_of(columns):
    return [
        pltpu.VMEM((32, 2, 16, columns), BF16),
        pltpu.VMEM((32, 16, columns), BF16),
        pltpu.VMEM((16, 2, 16, columns), BF16),
        pltpu.VMEM((16, 16, columns), BF16),
        pltpu.VMEM((16, 16, columns), BF16),
        pltpu.VMEM((16, 16, columns), BF16),
    ]


def per_device(events, out_grad, saved_attn, in_weight, out_weight, lengths):
    tile = (TOK, HD)
    vmem = pl.BlockSpec(memory_space=pltpu.VMEM)
    dma = pltpu.SemaphoreType.DMA
    scratch = [
        pltpu.VMEM((TOK, WIDTH), BF16),
        pltpu.VMEM(tile, BF16),
        pltpu.VMEM((WIDTH, 4 * HD), BF16),
        pltpu.VMEM((WIDTH, HD), BF16),
        pltpu.SMEM((NSEQ,), jnp.int32),
        pltpu.VMEM((HEADS,) + tile, F32),
        pltpu.VMEM((TOK, WIDTH), BF16),
        pltpu.VMEM((WIDTH, TOK), BF16),
        pltpu.VMEM(tile, F32),
        pltpu.VMEM((4,) + tile, F32),
        pltpu.VMEM(tile, F32),
        pltpu.VMEM(tile, F32),
        pltpu.VMEM(tile, F32),
        pltpu.VMEM((TOK, 4 * HD), BF16),
        pltpu.VMEM((HEADS,) + tile, BF16),
        pltpu.VMEM((REACH + 1,) + tile, BF16),
        pltpu.VMEM((REACH + 1,) + tile, BF16),
        pltpu.VMEM((4, 2) + tile, BF16),
        pltpu.VMEM((HD, 4 * TOK), BF16),
        pltpu.VMEM((REACH + 1, 8, TOK), jnp.int32),
        pltpu.VMEM((4 * TOK, HD), jnp.int32),
        pltpu.VMEM((4, 2) + tile, F32),
        pltpu.VMEM((REACH + 1, HD, TOK), BF16),
        pltpu.VMEM((REACH + 1, HD, TOK), BF16),
        pltpu.VMEM((2, 2) + tile, BF16),
        pltpu.VMEM((2, 2) + tile, BF16),
        pltpu.VMEM((2,) + tile, BF16),
        pltpu.VMEM((2,) + tile, BF16),
        *rows_of(2 * HD),
        *rows_of(3 * HD),
        pltpu.VMEM((HEADS,) + tile, BF16),
        pltpu.VMEM((HEADS,) + tile, BF16),
        pltpu.VMEM(tile, F32),
        pltpu.VMEM((8, TOK), F32),
        pltpu.VMEM((HEADS, 8, TOK), F32),
    ]
    counts = (8, 8, 5, 5, 5, 5, 4, 4, 5, 5, 2, 2, 3, 3, 16, 16, 3, 3, 16, 16, 8, 8, 8, 8)
    scratch += [dma((6,)), pltpu.SemaphoreType.REGULAR((3,))]
    scratch += [dma((n,)) for n in counts]
    return pl.pallas_call(
        kernel,
        out_shape=(
            jax.ShapeDtypeStruct(tile, BF16),
            jax.ShapeDtypeStruct((16, 4 * HD), F32),
            jax.ShapeDtypeStruct((16, HD), F32),
        ),
        in_specs=[pl.BlockSpec(memory_space=pl.ANY)] * 6,
        out_specs=(vmem,) * 3,
        scratch_shapes=scratch,
        compiler_params=pltpu.CompilerParams(
            collective_id=0, has_side_effects=True, vmem_limit_bytes=56 * 2**20
        ),
        name="layer_backward",
    )(events, out_grad, saved_attn, in_weight, out_weight, lengths)


def solution(mesh):
    return jax.shard_map(
        per_device,
        mesh=mesh,
        in_specs=(
            P("seq", None),
            P("seq", "head"),
            P("seq", "head"),
            P(None, "head"),
            P(None, "head"),
            P(),
        ),
        out_specs=(P("seq", "head"), P("seq", "head"), P("seq", "head")),
        check_vma=False,
    )
```

```python
import math

import jax
import jax.numpy as jnp
from jax import lax
from jax.experimental import pallas as pl
from jax.experimental.pallas import tpu as pltpu
from jax.sharding import PartitionSpec as P

HEADS = 8
HD = 128
TOK = 256
WIDTH = 1024
PLANES = 16
NSEQ = 16
REACH = 4
MOST = 4096.0
EPS = 1e-05
SCALE = 1.0 / math.sqrt(HD)
GRAD_SCALE = 1.0 / 128.0
MESH = pl.DeviceIdType.MESH
F32 = jnp.float32
BF16 = jnp.bfloat16
NEAR_LAST = (8, 7, 9, 6, 10, 5, 11, 4, 12, 3, 13, 2, 14, 1, 15)
FAR = 4
FAR_COUNT = 9


def nn(a, b):
    return jnp.dot(a, b, preferred_element_type=F32)


def nt(a, b):
    return lax.dot_general(a, b, (((1,), (1,)), ((), ())), preferred_element_type=F32)


def tn(a, b):
    return lax.dot_general(a, b, (((0,), (0,)), ((), ())), preferred_element_type=F32)


def push(src, dst, sent, came, device):
    return pltpu.make_async_remote_copy(
        src_ref=src,
        dst_ref=dst,
        send_sem=sent,
        recv_sem=came,
        device_id=device,
        device_id_type=MESH,
    )


def kernel(
    ev_h, og_h, sa_h, wi_h, wo_h, lens_h, gi, g1, g2,
    ev, sa, wi, wo, lens,
    n8, nb, ntr, rsd, slope, upart, ahat_s, arstd_s, dproj,
    fg, qa, doa, kva, ktr, begin, rowpos, kvg, dqs, dqr,
    kvs1, kvr1, kvs2, kvr2,
    ge, ge1, ga1, ge2, ga2, ge3,
    gl, gl1, gb1, gl2, gb2, gl3,
    ps, pr, own, st, sr,
    in_s, near,
    fg_s, fg_r, q_s, q_r, do_s, do_r, kv_s, kv_r, dq_s, dq_r, kx_s, kx_r,
    e12_s, e12_r, e3_s, e3_r, l12_s, l12_r, l3_s, l3_r, p_s, p_r, t_s, t_r,
):
    s = lax.axis_index("seq")
    h = lax.axis_index("head")
    z = s // 4
    xh = (s // 2) % 2
    c = s % 2

    def at_z(i):
        return (((z + i) % PLANES) * 4 + xh * 2 + c, h)

    def in_plane(i):
        return (z * 4 + ((xh + i // 2) % 2) * 2 + (c + i % 2) % 2, h)

    def at_head(i):
        return (s, (h + i) % HEADS)

    barrier = pltpu.get_barrier_semaphore()
    for i in range(1, HEADS):
        pl.semaphore_signal(barrier, inc=1, device_id=at_head(i), device_id_type=MESH)
    for i in range(1, 4):
        pl.semaphore_signal(barrier, inc=1, device_id=in_plane(i), device_id_type=MESH)
    for i in (1, PLANES - 1):
        pl.semaphore_signal(barrier, inc=1, device_id=at_z(i), device_id_type=MESH)

    def greet(level, distance):
        for i in (distance, PLANES - distance):
            pl.semaphore_signal(
                near.at[level], inc=1, device_id=at_z(i), device_id_type=MESH
            )

    loads = [
        pltpu.make_async_copy(src, dst, in_s.at[i])
        for i, (src, dst) in enumerate(
            ((og_h, fg.at[0]), (ev_h, ev), (wi_h, wi), (wo_h, wo), (sa_h, sa), (lens_h, lens))
        )
    ]
    for copy in loads:
        copy.start()

    def norm_rows(i, carry):
        r = pl.multiple_of(i * 64, 64)
        x = ev[pl.ds(r, 64), :].astype(F32)
        cent = x - jnp.mean(x, axis=1, keepdims=True)
        rstd = lax.rsqrt(jnp.mean(cent * cent, axis=1, keepdims=True) + EPS)
        normed = cent * rstd
        nb[pl.ds(r, 64), :] = normed.astype(BF16)
        for j in range(HEADS):
            n8[j, pl.ds(r, 64), :] = normed[:, j * HD : (j + 1) * HD]
        rsd[pl.ds(r, 64), :] = jnp.broadcast_to(rstd, (64, HD))
        return carry

    loads[1].wait()
    lax.fori_loop(0, 2, norm_rows, 0)

    loads[0].wait()
    pl.semaphore_wait(barrier, HEADS - 1 + 3 + 2)
    greet(0, 1)
    fg_copies = [
        push(fg.at[0], fg.at[i], fg_s.at[i], fg_r.at[i], at_head(i)) for i in range(1, HEADS)
    ]
    for i in (6, 2, 7, 5, 3, 1, 4):
        fg_copies[i - 1].start()

    lax.fori_loop(2, 4, norm_rows, 0)
    pl.semaphore_wait(near.at[0], 2)
    greet(1, 2)

    def hop_queries(d, by):
        return push(
            qa.at[d], qa.at[d + by], q_s.at[d + by], q_r.at[d + by], at_z(PLANES - by)
        )

    loads[2].wait()
    for part in (3, 1, 2, 0):
        proj = nn(nb[...], wi[:, part * HD : (part + 1) * HD])
        sig = 0.5 * jnp.tanh(0.5 * proj) + 0.5
        act = (proj * sig).astype(BF16)
        slope[part] = sig * (1.0 + proj * (1.0 - sig))
        if part == 0:
            upart[...] = act.astype(F32)
        elif part == 1:
            kva[0, 1] = act
        elif part == 2:
            qa[0] = act
        else:
            kva[0, 0] = act
        if part == 1:
            kv_copies = [
                push(kva.at[0], kva.at[i], kv_s.at[i], kv_r.at[i], in_plane(i))
                for i in (3, 2, 1)
            ]
            for copy in kv_copies:
                copy.start()
        elif part == 2:
            hop_queries(0, 2).start()
            hop_queries(0, 1).start()

    loads[4].wait()
    attn = sa[...].astype(F32)
    cent = attn - jnp.mean(attn, axis=1, keepdims=True)
    arstd = lax.rsqrt(jnp.mean(cent * cent, axis=1, keepdims=True) + EPS)
    ahat_s[...] = cent * arstd
    arstd_s[...] = jnp.broadcast_to(arstd, (TOK, HD))
    pl.semaphore_wait(near.at[1], 2)
    greet(2, 4)

    loads[3].wait()
    dout = nn(fg[0], wo[pl.ds(pl.multiple_of(h * HD, HD), HD), :])
    for i in (1, 7, 4, 2, 6, 3, 5):
        fg_copies[i - 1].wait_recv()
        row = pl.multiple_of(((h + HEADS - i) % HEADS) * HD, HD)
        dout += nn(fg[i], wo[pl.ds(row, HD), :])
    ahat = ahat_s[...]
    dnorm = dout * upart[...]
    doa[0] = (
        (
            dnorm
            - jnp.mean(dnorm, axis=1, keepdims=True)
            - ahat * jnp.mean(dnorm * ahat, axis=1, keepdims=True)
        )
        * arstd_s[...]
    ).astype(BF16)
    def hop_upstream(d, by):
        return push(
            doa.at[d], doa.at[d + by], do_s.at[d + by], do_r.at[d + by], at_z(PLANES - by)
        )

    hop_upstream(0, 2).start()
    hop_upstream(0, 1).start()
    hop_queries(0, 2).wait_recv()
    hop_queries(2, 2).start()
    hop_queries(0, 1).wait_recv()
    hop_queries(1, 2).start()

    def turn_columns(j, carry):
        ntr[pl.ds(pl.multiple_of(j * HD, HD), HD), :] = n8[j].T.astype(BF16)
        return carry

    lax.fori_loop(0, HEADS, turn_columns, 0)

    dproj[:, 0:HD] = (dout * ahat * slope[0]).astype(BF16)
    gated = (ahat * upart[...]).astype(BF16)
    ge[:, :, :, 0:HD] = (nn(ntr[...], dproj[:, 0:HD])).astype(BF16).reshape(32, 2, 16, HD)

    def head_rows(i, carry):
        block = pl.ds(((h + HEADS - i) % HEADS) * 4, 4)
        ge[block, :, :, HD : 2 * HD] = tn(fg[i], gated).astype(BF16).reshape(4, 2, 16, HD)
        return carry

    lax.fori_loop(0, HEADS, head_rows, 0)

    def sum_parts(whole, into, over):
        return push(whole.at[:, 1 - c], into, over[0].at[0], over[1].at[0], in_plane(1))

    def add_first(whole, came, kept):
        def step(k, carry):
            rows = pl.ds(2 * ((z + k + FAR) % PLANES), 2)
            kept[k] = (whole[rows, c].astype(F32) + came[rows].astype(F32)).astype(BF16)
            return carry

        lax.fori_loop(0, PLANES, step, 0)

    def sum_across(kept, into, over):
        return [
            push(
                kept.at[pl.ds(low, count), 1 - xh],
                into.at[pl.ds(low, count)],
                over[0].at[i],
                over[1].at[i],
                in_plane(2),
            )
            for i, low, count in ((1, 0, FAR_COUNT), (2, FAR_COUNT, PLANES - FAR_COUNT))
        ]

    def add_second(kept, came, final, low, high):
        def step(k, carry):
            final[k] = (kept[k, xh].astype(F32) + came[k].astype(F32)).astype(BF16)
            return carry

        lax.fori_loop(low, high, step, 0)

    def sum_planes(final, into, over):
        return [
            push(
                final.at[(i - FAR) % PLANES], into.at[i], over[0].at[i], over[1].at[i], at_z(i)
            )
            for i in NEAR_LAST
        ]

    def add_third(final, came):
        total = final[PLANES - FAR].astype(F32)
        for i in range(1, PLANES):
            total += came[i].astype(F32)
        return total * GRAD_SCALE

    e_first = sum_parts(ge, ge1, (e12_s, e12_r))
    e_first.start()

    loads[5].wait()
    ends = []
    run = 0
    for i in range(NSEQ):
        run = run + lens[i]
        ends.append(run)
    own_plane = (z + PLANES // 2) % PLANES

    def history_starts(d, carry):
        plane = own_plane + d
        qpos = plane * 1024 + xh * 512 + c * 256 + lax.broadcasted_iota(jnp.int32, (8, TOK), 1)
        first = jnp.zeros((8, TOK), jnp.int32)
        for end in ends:
            first = jnp.maximum(first, jnp.where(qpos >= end, end, 0))
        begin[d] = jnp.where(plane < PLANES, first - own_plane * 1024, 2 * 1024)
        return carry

    lax.fori_loop(0, REACH + 1, history_starts, 0)

    for copy in kv_copies:
        copy.wait_recv()
    for i in range(4):
        ktr[:, i * TOK : (i + 1) * TOK] = kva[i, 0].astype(F32).T.astype(BF16)

    def slot_rows(shape):
        row = lax.broadcasted_iota(jnp.int32, shape, 0)
        half = row // 512
        quarter = (row // 256) % 2
        place = jnp.where(xh == 0, half, 1 - half) * 512
        place += jnp.where(c == 0, quarter, 1 - quarter) * 256
        return place + row % 256

    rowpos[...] = slot_rows((4 * TOK, HD))
    kvg[...] = jnp.zeros_like(kvg)

    def attend(d):
        queries = qa[d]
        upstream = doa[d]
        keys = kva[:, 0].reshape(4 * TOK, HD)
        values = kva[:, 1].reshape(4 * TOK, HD)
        down = jnp.concatenate([rowpos[...]] * 2, axis=1)
        lane = lax.broadcasted_iota(jnp.int32, (1, TOK), 1)
        mask = (down >= begin[d, 0:1, :]) & (down <= d * 1024 + xh * 512 + c * 256 + lane)
        half = nt(keys, queries) * (0.5 * SCALE)
        bell = 1.0 + jnp.tanh(half)
        weight = half * bell
        sig = 0.5 * bell
        dprob = nt(values, upstream)
        dscore = jnp.where(mask, dprob * (sig + weight * (1.0 - sig)), 0.0).astype(BF16)
        weight = jnp.where(mask, weight, 0.0).astype(BF16)
        grad_k = nn(dscore, queries).reshape(4, TOK, HD)
        grad_v = nn(weight, upstream).reshape(4, TOK, HD)
        kvg[:, 0] += grad_k
        kvg[:, 1] += grad_v
        dqs[d] = nn(ktr[...], dscore).astype(BF16)

    hop_upstream(0, 2).wait_recv()
    hop_upstream(2, 2).start()
    hop_upstream(0, 1).wait_recv()
    hop_upstream(1, 2).start()
    e_second = sum_across(ga1, ge2, (e12_s, e12_r))

    def attend_step(turn, carry):
        d = jnp.where(turn < 3, 2 - turn, 7 - turn)

        @pl.when(d == 4)
        def _():
            hop_queries(2, 2).wait_recv()
            hop_upstream(2, 2).wait_recv()

        @pl.when(d == 3)
        def _():
            hop_queries(1, 2).wait_recv()
            hop_upstream(1, 2).wait_recv()

        attend(d)

        @pl.when(d > 0)
        def _():
            push(dqs.at[d], dqr.at[d], dq_s.at[d], dq_r.at[d], at_z(d)).start()

        @pl.when(d == 0)
        def _():
            e_first.wait_recv()
            add_first(ge, ge1, ga1)
            for copy in e_second:
                copy.start()

        return carry

    lax.fori_loop(0, REACH + 1, attend_step, 0)

    for j in range(2):
        other = 2 * j + 1
        kvs1[j] = kvg[other].astype(BF16)
    k_first = push(kvs1, kvr1, kx_s.at[0], kx_r.at[0], in_plane(1))
    k_first.start()


    k_first.wait_recv()
    kvs2[...] = (kvg[2] + kvr1[1].astype(F32)).astype(BF16)
    k_second = push(kvs2, kvr2, kx_s.at[1], kx_r.at[1], in_plane(2))
    k_second.start()

    for copy in e_second:
        copy.wait_recv()
    add_second(ga1, ge2, ga2, 0, PLANES)
    pl.semaphore_wait(near.at[2], 2)
    e_third = sum_planes(ga2, ge3, (e3_s, e3_r))
    dq_copies = [
        push(dqs.at[d], dqr.at[d], dq_s.at[d], dq_r.at[d], at_z(d)) for d in range(1, REACH + 1)
    ]
    k_second.wait_recv()
    grad_k = kvg[0, 0] + kvr1[0, 0].astype(F32) + kvr2[0].astype(F32)
    grad_v = kvg[0, 1] + kvr1[0, 1].astype(F32) + kvr2[1].astype(F32)
    dproj[:, 3 * HD :] = (grad_k * (SCALE / MOST) * slope[3]).astype(BF16)
    dproj[:, HD : 2 * HD] = (grad_v * (1.0 / MOST) * slope[1]).astype(BF16)
    pair = jnp.concatenate([dproj[:, HD : 2 * HD], dproj[:, 3 * HD :]], axis=1)
    gl[:, :, :, 0 : 2 * HD] = nn(ntr[...], pair).astype(BF16).reshape(32, 2, 16, 2 * HD)
    grad_q = dqs[0].astype(F32)
    for d in range(REACH, 0, -1):
        dq_copies[d - 1].wait_recv()
        grad_q += dqr[d].astype(F32)
    dproj[:, 2 * HD : 3 * HD] = (grad_q.T * (SCALE / MOST) * slope[2]).astype(BF16)
    gl[:, :, :, 2 * HD :] = (
        nn(ntr[...], dproj[:, 2 * HD : 3 * HD]).astype(BF16).reshape(32, 2, 16, HD)
    )

    l_first = sum_parts(gl, gl1, (l12_s, l12_r))
    l_first.start()
    for copy in e_third:
        copy.start()
    l_first.wait_recv()
    add_first(gl, gl1, gb1)
    l_second = sum_across(gb1, gl2, (l12_s, l12_r))
    for copy in l_second:
        copy.start()

    total = jnp.zeros((TOK, HD), F32)
    along = jnp.zeros((TOK, HD), F32)
    p_copies = []

    def spread(i, total, along):
        hh = (h + i) % HEADS
        part = nt(dproj[...], wi[pl.ds(pl.multiple_of(hh * HD, HD), HD), :])
        if i:
            ps[i] = part.astype(BF16)
            copy = push(ps.at[i], pr.at[i], p_s.at[i], p_r.at[i], at_head(i))
            copy.start()
            p_copies.append((i, copy))
        else:
            own[...] = part
        return total + part, along + part * n8[hh]

    for i in (6, 2, 7, 5, 3, 1, 4, 0):
        total, along = spread(i, total, along)
    lane = lax.broadcasted_iota(jnp.int32, (TOK, HD), 1)
    both = jnp.where(
        lane == 0,
        jnp.sum(total, axis=1, keepdims=True),
        jnp.where(lane == 1, jnp.sum(along, axis=1, keepdims=True), 0.0),
    )
    st[...] = both.T[0:8, :]
    t_copies = [
        push(st, sr.at[i], t_s.at[i], t_r.at[i], at_head(i)) for i in range(1, HEADS)
    ]
    for copy in t_copies:
        copy.start()

    l_third = sum_planes(gb2, gl3, (l3_s, l3_r))
    l_second[0].wait_recv()
    add_second(gb1, gl2, gb2, 0, FAR_COUNT)
    for copy in l_third[:FAR_COUNT]:
        copy.start()
    l_second[1].wait_recv()
    add_second(gb1, gl2, gb2, FAR_COUNT, PLANES)
    for copy in l_third[FAR_COUNT:]:
        copy.start()

    for copy in e_third:
        copy.wait_recv()
    early = add_third(ga2, ge3)
    g1[:, 0:HD] = early[:, 0:HD]
    g2[...] = early[:, HD:]

    summed = own[...]
    for i, copy in p_copies:
        copy.wait_recv()
        summed += pr[i].astype(F32)
    stats = st[...]
    for i in range(1, HEADS):
        t_copies[i - 1].wait_recv()
        stats += sr[i]
    wide = jnp.concatenate([stats, jnp.zeros((HD - 8, TOK), F32)], axis=0).T * (1.0 / WIDTH)
    back = (summed - wide[:, 0:1] - n8[h] * wide[:, 1:2]) * rsd[...]
    gi[...] = (fg[0].astype(F32) + back).astype(BF16)

    for copy in (
        fg_copies + kv_copies + dq_copies + e_third + t_copies
    ):
        copy.wait_send()
    for d, by in ((0, 1), (0, 2), (1, 2), (2, 2)):
        hop_queries(d, by).wait_send()
        hop_upstream(d, by).wait_send()
    for i, copy in p_copies:
        copy.wait_send()
    for copy in e_second + l_second + [e_first, k_first, k_second, l_first]:
        copy.wait_send()

    for copy in l_third:
        copy.wait_recv()
    late = add_third(gb2, gl3)
    g1[:, HD : 2 * HD] = late[:, 0:HD]
    g1[:, 2 * HD : 3 * HD] = late[:, 2 * HD :]
    g1[:, 3 * HD :] = late[:, HD : 2 * HD]
    for copy in l_third:
        copy.wait_send()


def rows_of(columns):
    return [
        pltpu.VMEM((32, 2, 16, columns), BF16),
        pltpu.VMEM((32, 16, columns), BF16),
        pltpu.VMEM((16, 2, 16, columns), BF16),
        pltpu.VMEM((16, 16, columns), BF16),
        pltpu.VMEM((16, 16, columns), BF16),
        pltpu.VMEM((16, 16, columns), BF16),
    ]


def per_device(events, out_grad, saved_attn, in_weight, out_weight, lengths):
    tile = (TOK, HD)
    vmem = pl.BlockSpec(memory_space=pltpu.VMEM)
    dma = pltpu.SemaphoreType.DMA
    scratch = [
        pltpu.VMEM((TOK, WIDTH), BF16),
        pltpu.VMEM(tile, BF16),
        pltpu.VMEM((WIDTH, 4 * HD), BF16),
        pltpu.VMEM((WIDTH, HD), BF16),
        pltpu.SMEM((NSEQ,), jnp.int32),
        pltpu.VMEM((HEADS,) + tile, F32),
        pltpu.VMEM((TOK, WIDTH), BF16),
        pltpu.VMEM((WIDTH, TOK), BF16),
        pltpu.VMEM(tile, F32),
        pltpu.VMEM((4,) + tile, F32),
        pltpu.VMEM(tile, F32),
        pltpu.VMEM(tile, F32),
        pltpu.VMEM(tile, F32),
        pltpu.VMEM((TOK, 4 * HD), BF16),
        pltpu.VMEM((HEADS,) + tile, BF16),
        pltpu.VMEM((REACH + 1,) + tile, BF16),
        pltpu.VMEM((REACH + 1,) + tile, BF16),
        pltpu.VMEM((4, 2) + tile, BF16),
        pltpu.VMEM((HD, 4 * TOK), BF16),
        pltpu.VMEM((REACH + 1, 8, TOK), jnp.int32),
        pltpu.VMEM((4 * TOK, HD), jnp.int32),
        pltpu.VMEM((4, 2) + tile, F32),
        pltpu.VMEM((REACH + 1, HD, TOK), BF16),
        pltpu.VMEM((REACH + 1, HD, TOK), BF16),
        pltpu.VMEM((2, 2) + tile, BF16),
        pltpu.VMEM((2, 2) + tile, BF16),
        pltpu.VMEM((2,) + tile, BF16),
        pltpu.VMEM((2,) + tile, BF16),
        *rows_of(2 * HD),
        *rows_of(3 * HD),
        pltpu.VMEM((HEADS,) + tile, BF16),
        pltpu.VMEM((HEADS,) + tile, BF16),
        pltpu.VMEM(tile, F32),
        pltpu.VMEM((8, TOK), F32),
        pltpu.VMEM((HEADS, 8, TOK), F32),
    ]
    counts = (8, 8, 5, 5, 5, 5, 4, 4, 5, 5, 2, 2, 3, 3, 16, 16, 3, 3, 16, 16, 8, 8, 8, 8)
    scratch += [dma((6,)), pltpu.SemaphoreType.REGULAR((3,))]
    scratch += [dma((n,)) for n in counts]
    return pl.pallas_call(
        kernel,
        out_shape=(
            jax.ShapeDtypeStruct(tile, BF16),
            jax.ShapeDtypeStruct((16, 4 * HD), F32),
            jax.ShapeDtypeStruct((16, HD), F32),
        ),
        in_specs=[pl.BlockSpec(memory_space=pl.ANY)] * 6,
        out_specs=(vmem,) * 3,
        scratch_shapes=scratch,
        compiler_params=pltpu.CompilerParams(
            collective_id=0, has_side_effects=True, vmem_limit_bytes=56 * 2**20
        ),
        name="layer_backward",
    )(events, out_grad, saved_attn, in_weight, out_weight, lengths)


def solution(mesh):
    return jax.shard_map(
        per_device,
        mesh=mesh,
        in_specs=(
            P("seq", None),
            P("seq", "head"),
            P("seq", "head"),
            P(None, "head"),
            P(None, "head"),
            P(),
        ),
        out_specs=(P("seq", "head"), P("seq", "head"), P("seq", "head")),
        check_vma=False,
    )
```

```python
import math

import jax
import jax.numpy as jnp
from jax import lax
from jax.experimental import pallas as pl
from jax.experimental.pallas import tpu as pltpu
from jax.sharding import PartitionSpec as P

HEADS = 8
HD = 128
TOK = 256
WIDTH = 1024
PLANES = 16
NSEQ = 16
REACH = 4
MOST = 4096.0
EPS = 1e-05
SCALE = 1.0 / math.sqrt(HD)
GRAD_SCALE = 1.0 / 128.0
MESH = pl.DeviceIdType.MESH
F32 = jnp.float32
BF16 = jnp.bfloat16
NEAR_LAST = (8, 7, 9, 6, 10, 5, 11, 4, 12, 3, 13, 2, 14, 1, 15)
FAR = 4
FAR_COUNT = 9


def nn(a, b):
    return jnp.dot(a, b, preferred_element_type=F32)


def nt(a, b):
    return lax.dot_general(a, b, (((1,), (1,)), ((), ())), preferred_element_type=F32)


def tn(a, b):
    return lax.dot_general(a, b, (((0,), (0,)), ((), ())), preferred_element_type=F32)


def push(src, dst, sent, came, device):
    return pltpu.make_async_remote_copy(
        src_ref=src,
        dst_ref=dst,
        send_sem=sent,
        recv_sem=came,
        device_id=device,
        device_id_type=MESH,
    )


def kernel(
    ev_h, og_h, sa_h, wi_h, wo_h, lens_h, gi, g1, g2,
    ev, sa, wi, wo, lens,
    n8, nb, ntr, rsd, slope, upart, ahat_s, arstd_s, dproj,
    fg, qa, doa, kva, ktr, begin, rowpos, kvg, dqs, dqr,
    kvs1, kvr1, kvs2, kvr2,
    ge, ge1, ga1, ge2, ga2, ge3,
    gl, gl1, gb1, gl2, gq, gq1, gc1, gq2, gb2, gl3,
    ps, pr, own, st, sr,
    in_s, near,
    fg_s, fg_r, q_s, q_r, do_s, do_r, kv_s, kv_r, dq_s, dq_r, kx_s, kx_r,
    e12_s, e12_r, e3_s, e3_r, l12_s, l12_r, c12_s, c12_r, l3_s, l3_r, p_s, p_r, t_s, t_r,
):
    s = lax.axis_index("seq")
    h = lax.axis_index("head")
    z = s // 4
    xh = (s // 2) % 2
    c = s % 2

    def at_z(i):
        return (((z + i) % PLANES) * 4 + xh * 2 + c, h)

    def in_plane(i):
        return (z * 4 + ((xh + i // 2) % 2) * 2 + (c + i % 2) % 2, h)

    def at_head(i):
        return (s, (h + i) % HEADS)

    barrier = pltpu.get_barrier_semaphore()
    for i in range(1, HEADS):
        pl.semaphore_signal(barrier, inc=1, device_id=at_head(i), device_id_type=MESH)
    for i in range(1, 4):
        pl.semaphore_signal(barrier, inc=1, device_id=in_plane(i), device_id_type=MESH)
    for i in (1, PLANES - 1):
        pl.semaphore_signal(barrier, inc=1, device_id=at_z(i), device_id_type=MESH)

    def greet(level, distance):
        for i in (distance, PLANES - distance):
            pl.semaphore_signal(
                near.at[level], inc=1, device_id=at_z(i), device_id_type=MESH
            )

    loads = [
        pltpu.make_async_copy(src, dst, in_s.at[i])
        for i, (src, dst) in enumerate(
            ((og_h, fg.at[0]), (ev_h, ev), (wi_h, wi), (wo_h, wo), (sa_h, sa), (lens_h, lens))
        )
    ]
    for copy in loads:
        copy.start()

    def norm_rows(i, carry):
        r = pl.multiple_of(i * 64, 64)
        x = ev[pl.ds(r, 64), :].astype(F32)
        cent = x - jnp.mean(x, axis=1, keepdims=True)
        rstd = lax.rsqrt(jnp.mean(cent * cent, axis=1, keepdims=True) + EPS)
        normed = cent * rstd
        nb[pl.ds(r, 64), :] = normed.astype(BF16)
        for j in range(HEADS):
            n8[j, pl.ds(r, 64), :] = normed[:, j * HD : (j + 1) * HD]
        rsd[pl.ds(r, 64), :] = jnp.broadcast_to(rstd, (64, HD))
        return carry

    loads[1].wait()
    lax.fori_loop(0, 2, norm_rows, 0)

    loads[0].wait()
    pl.semaphore_wait(barrier, HEADS - 1 + 3 + 2)
    greet(0, 1)
    fg_copies = [
        push(fg.at[0], fg.at[i], fg_s.at[i], fg_r.at[i], at_head(i)) for i in range(1, HEADS)
    ]
    for i in (6, 2, 7, 5, 3, 1, 4):
        fg_copies[i - 1].start()

    lax.fori_loop(2, 4, norm_rows, 0)
    pl.semaphore_wait(near.at[0], 2)
    greet(1, 2)

    def hop_queries(d, by):
        return push(
            qa.at[d], qa.at[d + by], q_s.at[d + by], q_r.at[d + by], at_z(PLANES - by)
        )

    loads[2].wait()
    for part in (3, 1, 2, 0):
        proj = nn(nb[...], wi[:, part * HD : (part + 1) * HD])
        sig = 0.5 * jnp.tanh(0.5 * proj) + 0.5
        act = (proj * sig).astype(BF16)
        slope[part] = sig * (1.0 + proj * (1.0 - sig))
        if part == 0:
            upart[...] = act.astype(F32)
        elif part == 1:
            kva[0, 1] = act
        elif part == 2:
            qa[0] = act
        else:
            kva[0, 0] = act
        if part == 1:
            kv_copies = [
                push(kva.at[0], kva.at[i], kv_s.at[i], kv_r.at[i], in_plane(i))
                for i in (3, 2, 1)
            ]
            for copy in kv_copies:
                copy.start()
        elif part == 2:
            hop_queries(0, 2).start()
            hop_queries(0, 1).start()

    loads[4].wait()
    attn = sa[...].astype(F32)
    cent = attn - jnp.mean(attn, axis=1, keepdims=True)
    arstd = lax.rsqrt(jnp.mean(cent * cent, axis=1, keepdims=True) + EPS)
    ahat_s[...] = cent * arstd
    arstd_s[...] = jnp.broadcast_to(arstd, (TOK, HD))
    pl.semaphore_wait(near.at[1], 2)
    greet(2, 4)

    loads[3].wait()
    dout = nn(fg[0], wo[pl.ds(pl.multiple_of(h * HD, HD), HD), :])
    for i in (1, 7, 4, 2, 6, 3, 5):
        fg_copies[i - 1].wait_recv()
        row = pl.multiple_of(((h + HEADS - i) % HEADS) * HD, HD)
        dout += nn(fg[i], wo[pl.ds(row, HD), :])
    ahat = ahat_s[...]
    dnorm = dout * upart[...]
    doa[0] = (
        (
            dnorm
            - jnp.mean(dnorm, axis=1, keepdims=True)
            - ahat * jnp.mean(dnorm * ahat, axis=1, keepdims=True)
        )
        * arstd_s[...]
    ).astype(BF16)
    def hop_upstream(d, by):
        return push(
            doa.at[d], doa.at[d + by], do_s.at[d + by], do_r.at[d + by], at_z(PLANES - by)
        )

    hop_upstream(0, 2).start()
    hop_upstream(0, 1).start()
    hop_queries(0, 2).wait_recv()
    hop_queries(2, 2).start()
    hop_queries(0, 1).wait_recv()
    hop_queries(1, 2).start()

    def turn_columns(j, carry):
        ntr[pl.ds(pl.multiple_of(j * HD, HD), HD), :] = n8[j].T.astype(BF16)
        return carry

    lax.fori_loop(0, HEADS, turn_columns, 0)

    dproj[:, 0:HD] = (dout * ahat * slope[0]).astype(BF16)
    gated = (ahat * upart[...]).astype(BF16)
    ge[:, :, :, 0:HD] = (nn(ntr[...], dproj[:, 0:HD])).astype(BF16).reshape(32, 2, 16, HD)

    def head_rows(i, carry):
        block = pl.ds(((h + HEADS - i) % HEADS) * 4, 4)
        ge[block, :, :, HD : 2 * HD] = tn(fg[i], gated).astype(BF16).reshape(4, 2, 16, HD)
        return carry

    lax.fori_loop(0, HEADS, head_rows, 0)

    def sum_parts(whole, into, over):
        return push(whole.at[:, 1 - c], into, over[0].at[0], over[1].at[0], in_plane(1))

    def add_first(whole, came, kept):
        def step(k, carry):
            rows = pl.ds(2 * ((z + k + FAR) % PLANES), 2)
            kept[k] = (whole[rows, c].astype(F32) + came[rows].astype(F32)).astype(BF16)
            return carry

        lax.fori_loop(0, PLANES, step, 0)

    def sum_across(kept, into, over):
        return [
            push(
                kept.at[pl.ds(low, count), 1 - xh],
                into.at[pl.ds(low, count)],
                over[0].at[i],
                over[1].at[i],
                in_plane(2),
            )
            for i, low, count in ((1, 0, FAR_COUNT), (2, FAR_COUNT, PLANES - FAR_COUNT))
        ]

    def add_second(kept, came, final, low, high, left=0):
        def step(k, carry):
            final[k, :, left : left + kept.shape[3]] = (
                kept[k, xh].astype(F32) + came[k].astype(F32)
            ).astype(BF16)
            return carry

        lax.fori_loop(low, high, step, 0)

    def sum_planes(final, into, over):
        return [
            push(
                final.at[(i - FAR) % PLANES], into.at[i], over[0].at[i], over[1].at[i], at_z(i)
            )
            for i in NEAR_LAST
        ]

    def add_third(final, came):
        total = final[PLANES - FAR].astype(F32)
        for i in range(1, PLANES):
            total += came[i].astype(F32)
        return total * GRAD_SCALE

    e_first = sum_parts(ge, ge1, (e12_s, e12_r))
    e_first.start()

    loads[5].wait()
    ends = []
    run = 0
    for i in range(NSEQ):
        run = run + lens[i]
        ends.append(run)
    own_plane = (z + PLANES // 2) % PLANES

    def history_starts(d, carry):
        plane = own_plane + d
        qpos = plane * 1024 + xh * 512 + c * 256 + lax.broadcasted_iota(jnp.int32, (8, TOK), 1)
        first = jnp.zeros((8, TOK), jnp.int32)
        for end in ends:
            first = jnp.maximum(first, jnp.where(qpos >= end, end, 0))
        begin[d] = jnp.where(plane < PLANES, first - own_plane * 1024, 2 * 1024)
        return carry

    lax.fori_loop(0, REACH + 1, history_starts, 0)

    for copy in kv_copies:
        copy.wait_recv()
    for i in range(4):
        ktr[:, i * TOK : (i + 1) * TOK] = kva[i, 0].astype(F32).T.astype(BF16)

    def slot_rows(shape):
        row = lax.broadcasted_iota(jnp.int32, shape, 0)
        half = row // 512
        quarter = (row // 256) % 2
        place = jnp.where(xh == 0, half, 1 - half) * 512
        place += jnp.where(c == 0, quarter, 1 - quarter) * 256
        return place + row % 256

    rowpos[...] = slot_rows((4 * TOK, HD))
    kvg[...] = jnp.zeros_like(kvg)

    def attend(d):
        queries = qa[d]
        upstream = doa[d]
        keys = kva[:, 0].reshape(4 * TOK, HD)
        values = kva[:, 1].reshape(4 * TOK, HD)
        down = jnp.concatenate([rowpos[...]] * 2, axis=1)
        lane = lax.broadcasted_iota(jnp.int32, (1, TOK), 1)
        mask = (down >= begin[d, 0:1, :]) & (down <= d * 1024 + xh * 512 + c * 256 + lane)
        half = nt(keys, queries) * (0.5 * SCALE)
        bell = 1.0 + jnp.tanh(half)
        weight = half * bell
        sig = 0.5 * bell
        dprob = nt(values, upstream)
        dscore = jnp.where(mask, dprob * (sig + weight * (1.0 - sig)), 0.0).astype(BF16)
        weight = jnp.where(mask, weight, 0.0).astype(BF16)
        grad_k = nn(dscore, queries).reshape(4, TOK, HD)
        grad_v = nn(weight, upstream).reshape(4, TOK, HD)
        kvg[:, 0] += grad_k
        kvg[:, 1] += grad_v
        dqs[d] = nn(ktr[...], dscore).astype(BF16)

    hop_upstream(0, 2).wait_recv()
    hop_upstream(2, 2).start()
    hop_upstream(0, 1).wait_recv()
    hop_upstream(1, 2).start()
    e_second = sum_across(ga1, ge2, (e12_s, e12_r))

    def attend_step(turn, carry):
        d = jnp.where(turn < 3, 2 - turn, 7 - turn)

        @pl.when(d == 4)
        def _():
            hop_queries(2, 2).wait_recv()
            hop_upstream(2, 2).wait_recv()

        @pl.when(d == 3)
        def _():
            hop_queries(1, 2).wait_recv()
            hop_upstream(1, 2).wait_recv()

        attend(d)

        @pl.when(d > 0)
        def _():
            push(dqs.at[d], dqr.at[d], dq_s.at[d], dq_r.at[d], at_z(d)).start()

        @pl.when(d == 0)
        def _():
            e_first.wait_recv()
            add_first(ge, ge1, ga1)
            for copy in e_second:
                copy.start()

        return carry

    lax.fori_loop(0, REACH + 1, attend_step, 0)

    for j in range(2):
        other = 2 * j + 1
        kvs1[j] = kvg[other].astype(BF16)
    k_first = push(kvs1, kvr1, kx_s.at[0], kx_r.at[0], in_plane(1))
    k_first.start()


    k_first.wait_recv()
    kvs2[...] = (kvg[2] + kvr1[1].astype(F32)).astype(BF16)
    k_second = push(kvs2, kvr2, kx_s.at[1], kx_r.at[1], in_plane(2))
    k_second.start()

    for copy in e_second:
        copy.wait_recv()
    add_second(ga1, ge2, ga2, 0, PLANES)
    pl.semaphore_wait(near.at[2], 2)
    e_third = sum_planes(ga2, ge3, (e3_s, e3_r))
    dq_copies = [
        push(dqs.at[d], dqr.at[d], dq_s.at[d], dq_r.at[d], at_z(d)) for d in range(1, REACH + 1)
    ]
    k_second.wait_recv()
    grad_k = kvg[0, 0] + kvr1[0, 0].astype(F32) + kvr2[0].astype(F32)
    grad_v = kvg[0, 1] + kvr1[0, 1].astype(F32) + kvr2[1].astype(F32)
    dproj[:, 3 * HD :] = (grad_k * (SCALE / MOST) * slope[3]).astype(BF16)
    dproj[:, HD : 2 * HD] = (grad_v * (1.0 / MOST) * slope[1]).astype(BF16)
    pair = jnp.concatenate([dproj[:, HD : 2 * HD], dproj[:, 3 * HD :]], axis=1)
    gl[...] = nn(ntr[...], pair).astype(BF16).reshape(32, 2, 16, 2 * HD)
    l_first = sum_parts(gl, gl1, (l12_s, l12_r))
    l_first.start()
    l_first.wait_recv()
    add_first(gl, gl1, gb1)
    l_second = sum_across(gb1, gl2, (l12_s, l12_r))
    for copy in l_second:
        copy.start()
    grad_q = dqs[0].astype(F32)
    for d in range(REACH, 0, -1):
        dq_copies[d - 1].wait_recv()
        grad_q += dqr[d].astype(F32)
    dproj[:, 2 * HD : 3 * HD] = (grad_q.T * (SCALE / MOST) * slope[2]).astype(BF16)
    gq[...] = nn(ntr[...], dproj[:, 2 * HD : 3 * HD]).astype(BF16).reshape(32, 2, 16, HD)
    q_first = sum_parts(gq, gq1, (c12_s, c12_r))
    q_first.start()
    for copy in e_third:
        copy.start()
    q_first.wait_recv()
    add_first(gq, gq1, gc1)
    q_second = sum_across(gc1, gq2, (c12_s, c12_r))
    for copy in q_second:
        copy.start()

    total = jnp.zeros((TOK, HD), F32)
    along = jnp.zeros((TOK, HD), F32)
    p_copies = []

    def spread(i, total, along):
        hh = (h + i) % HEADS
        part = nt(dproj[...], wi[pl.ds(pl.multiple_of(hh * HD, HD), HD), :])
        if i:
            ps[i] = part.astype(BF16)
            copy = push(ps.at[i], pr.at[i], p_s.at[i], p_r.at[i], at_head(i))
            copy.start()
            p_copies.append((i, copy))
        else:
            own[...] = part
        return total + part, along + part * n8[hh]

    for i in (6, 2, 7, 5, 3, 1, 4, 0):
        total, along = spread(i, total, along)
    lane = lax.broadcasted_iota(jnp.int32, (TOK, HD), 1)
    both = jnp.where(
        lane == 0,
        jnp.sum(total, axis=1, keepdims=True),
        jnp.where(lane == 1, jnp.sum(along, axis=1, keepdims=True), 0.0),
    )
    st[...] = both.T[0:8, :]
    t_copies = [
        push(st, sr.at[i], t_s.at[i], t_r.at[i], at_head(i)) for i in range(1, HEADS)
    ]
    for copy in t_copies:
        copy.start()

    l_third = sum_planes(gb2, gl3, (l3_s, l3_r))
    for copy in l_second:
        copy.wait_recv()
    add_second(gb1, gl2, gb2, 0, PLANES)
    q_second[0].wait_recv()
    add_second(gc1, gq2, gb2, 0, FAR_COUNT, 2 * HD)
    for copy in l_third[:FAR_COUNT]:
        copy.start()
    q_second[1].wait_recv()
    add_second(gc1, gq2, gb2, FAR_COUNT, PLANES, 2 * HD)
    for copy in l_third[FAR_COUNT:]:
        copy.start()

    for copy in e_third:
        copy.wait_recv()
    early = add_third(ga2, ge3)
    g1[:, 0:HD] = early[:, 0:HD]
    g2[...] = early[:, HD:]

    summed = own[...]
    for i, copy in p_copies:
        copy.wait_recv()
        summed += pr[i].astype(F32)
    stats = st[...]
    for i in range(1, HEADS):
        t_copies[i - 1].wait_recv()
        stats += sr[i]
    wide = jnp.concatenate([stats, jnp.zeros((HD - 8, TOK), F32)], axis=0).T * (1.0 / WIDTH)
    back = (summed - wide[:, 0:1] - n8[h] * wide[:, 1:2]) * rsd[...]
    gi[...] = (fg[0].astype(F32) + back).astype(BF16)

    for copy in (
        fg_copies + kv_copies + dq_copies + e_third + t_copies
    ):
        copy.wait_send()
    for d, by in ((0, 1), (0, 2), (1, 2), (2, 2)):
        hop_queries(d, by).wait_send()
        hop_upstream(d, by).wait_send()
    for i, copy in p_copies:
        copy.wait_send()
    for copy in e_second + l_second + q_second + [e_first, k_first, k_second, l_first, q_first]:
        copy.wait_send()

    for copy in l_third:
        copy.wait_recv()
    late = add_third(gb2, gl3)
    g1[:, HD : 2 * HD] = late[:, 0:HD]
    g1[:, 2 * HD : 3 * HD] = late[:, 2 * HD :]
    g1[:, 3 * HD :] = late[:, HD : 2 * HD]
    for copy in l_third:
        copy.wait_send()


def rows_of(columns):
    return [
        pltpu.VMEM((32, 2, 16, columns), BF16),
        pltpu.VMEM((32, 16, columns), BF16),
        pltpu.VMEM((16, 2, 16, columns), BF16),
        pltpu.VMEM((16, 16, columns), BF16),
        pltpu.VMEM((16, 16, columns), BF16),
        pltpu.VMEM((16, 16, columns), BF16),
    ]


def per_device(events, out_grad, saved_attn, in_weight, out_weight, lengths):
    tile = (TOK, HD)
    vmem = pl.BlockSpec(memory_space=pltpu.VMEM)
    dma = pltpu.SemaphoreType.DMA
    scratch = [
        pltpu.VMEM((TOK, WIDTH), BF16),
        pltpu.VMEM(tile, BF16),
        pltpu.VMEM((WIDTH, 4 * HD), BF16),
        pltpu.VMEM((WIDTH, HD), BF16),
        pltpu.SMEM((NSEQ,), jnp.int32),
        pltpu.VMEM((HEADS,) + tile, F32),
        pltpu.VMEM((TOK, WIDTH), BF16),
        pltpu.VMEM((WIDTH, TOK), BF16),
        pltpu.VMEM(tile, F32),
        pltpu.VMEM((4,) + tile, F32),
        pltpu.VMEM(tile, F32),
        pltpu.VMEM(tile, F32),
        pltpu.VMEM(tile, F32),
        pltpu.VMEM((TOK, 4 * HD), BF16),
        pltpu.VMEM((HEADS,) + tile, BF16),
        pltpu.VMEM((REACH + 1,) + tile, BF16),
        pltpu.VMEM((REACH + 1,) + tile, BF16),
        pltpu.VMEM((4, 2) + tile, BF16),
        pltpu.VMEM((HD, 4 * TOK), BF16),
        pltpu.VMEM((REACH + 1, 8, TOK), jnp.int32),
        pltpu.VMEM((4 * TOK, HD), jnp.int32),
        pltpu.VMEM((4, 2) + tile, F32),
        pltpu.VMEM((REACH + 1, HD, TOK), BF16),
        pltpu.VMEM((REACH + 1, HD, TOK), BF16),
        pltpu.VMEM((2, 2) + tile, BF16),
        pltpu.VMEM((2, 2) + tile, BF16),
        pltpu.VMEM((2,) + tile, BF16),
        pltpu.VMEM((2,) + tile, BF16),
        *rows_of(2 * HD),
        *rows_of(2 * HD)[:4],
        *rows_of(HD)[:4],
        *rows_of(3 * HD)[4:],
        pltpu.VMEM((HEADS,) + tile, BF16),
        pltpu.VMEM((HEADS,) + tile, BF16),
        pltpu.VMEM(tile, F32),
        pltpu.VMEM((8, TOK), F32),
        pltpu.VMEM((HEADS, 8, TOK), F32),
    ]
    counts = (8, 8, 5, 5, 5, 5, 4, 4, 5, 5, 2, 2, 3, 3, 16, 16, 3, 3, 3, 3, 16, 16, 8, 8, 8, 8)
    scratch += [dma((6,)), pltpu.SemaphoreType.REGULAR((3,))]
    scratch += [dma((n,)) for n in counts]
    return pl.pallas_call(
        kernel,
        out_shape=(
            jax.ShapeDtypeStruct(tile, BF16),
            jax.ShapeDtypeStruct((16, 4 * HD), F32),
            jax.ShapeDtypeStruct((16, HD), F32),
        ),
        in_specs=[pl.BlockSpec(memory_space=pl.ANY)] * 6,
        out_specs=(vmem,) * 3,
        scratch_shapes=scratch,
        compiler_params=pltpu.CompilerParams(
            collective_id=0, has_side_effects=True, vmem_limit_bytes=56 * 2**20
        ),
        name="layer_backward",
    )(events, out_grad, saved_attn, in_weight, out_weight, lengths)


def solution(mesh):
    return jax.shard_map(
        per_device,
        mesh=mesh,
        in_specs=(
            P("seq", None),
            P("seq", "head"),
            P("seq", "head"),
            P(None, "head"),
            P(None, "head"),
            P(),
        ),
        out_specs=(P("seq", "head"), P("seq", "head"), P("seq", "head")),
        check_vma=False,
    )
```
